512 devices in a mesh: dp: 64 (over x, y, z_hi), mp: 8 (over z_lo, core).
Axes of the slice: x: 4, y: 8, z: 8 (z_hi: 2, z_lo: 4; z = z_hi * 4 + z_lo), core: 2. Of those that a mesh axis runs over, the one named last changes fastest.
Arguments:
- layer_input: bfloat16 [32768, 1280], P('dp', 'mp'), may hold values from -6 to 6
- first_weight: bfloat16 [1280, 5120], P(None, 'mp'), may hold values from -0.15625 to 0.15625
- first_bias: float32 [5120], P('mp'), may hold values from -3 to 3
- hidden_grad: bfloat16 [32768, 5120], P('dp', 'mp'), may hold values from -51 to 51
- other_squares: float32 [128], P('dp'), may hold values from 0.05 to 1
- weight_noise: float32 [1280, 5120], P('dp', 'mp'), may hold values from -96 to 96
- bias_noise: float32 [5120], P('mp'), may hold values from -96 to 96
Outputs:
- input_grad: bfloat16 [32768, 1280], P('dp', 'mp')
- weight_grad: float32 [1280, 5120], P('dp', 'mp')
- bias_grad: float32 [5120], P('mp')
The draws below stay inside these ranges and needn't reach their ends.
All inputs are finite; a program needn't handle non-finite values.
Results may differ from the reference program's by a relative error of at most 0.017.
Values may be sent and summed in bfloat16 or wider, within the bound.
A program may use at most 64 MiB of HBM per device.

```python
import math
import jax
import jax.numpy as jnp
from jax import lax

D = 1280
FF = 5120
SEQ = 256
EXAMPLES = 128
TOKENS = 32768
N_MP = 8


def draw_hidden_grad(key, part):
    key = jax.random.fold_in(key, 11)
    key_example = jax.random.fold_in(key, 0)
    key_token = jax.random.fold_in(key, 1)
    key_value = jax.random.fold_in(key, 3)
    examples = TOKENS // SEQ
    example_scale = jnp.exp(jax.random.uniform(key_example, (examples, 1, 1), jnp.float32, math.log(0.3), math.log(3.0)))
    token_scale = jnp.exp2(jax.random.uniform(key_token, (examples, SEQ, 1), jnp.float32, -1.0, 1.0))
    column_scale = jnp.exp(jnp.arange(FF, dtype=jnp.float32).reshape(1, 1, FF) * (math.log(10.0) / FF))
    values = jax.random.truncated_normal(key_value, -3.0, 3.0, (examples, SEQ, FF), jnp.float32)
    result = 0.28 * values * example_scale * token_scale * column_scale
    return result.reshape(TOKENS, FF).astype(jnp.bfloat16)


def shard_levels(stream_key, extent, cuts, smallest, high):
    def one(position, parts):
        draws = jax.random.uniform(jax.random.fold_in(jax.random.fold_in(stream_key, 6), position), (parts,), jnp.float32, smallest / len(cuts), high / len(cuts))
        return jnp.repeat(jnp.exp(draws), extent[position] // parts).reshape((-1,) + (1,) * (len(extent) - position - 1))

    gain = one(*cuts[0])
    for cut in cuts[1:]:
        gain = gain * one(*cut)
    return gain


def scatter_about(own_key, shape, spread, most, cuts=(), kind=jnp.bfloat16):
    level = shard_levels(own_key, shape, cuts, -0.22, 0.18) if cuts else 1.0
    array = jax.random.normal(own_key, shape, jnp.float32) * spread * level
    return jnp.minimum(jnp.maximum(array, -most), most).astype(kind)


def setup_inputs(seed: int = 0) -> dict:
    splits = jax.random.split(jax.random.key(seed), 8)
    return {
        "layer_input": scatter_about(splits[0], (TOKENS, D), 1.0, 6.0, ((0, 64), (1, 8))),
        "first_weight": scatter_about(splits[1], (D, FF), D ** -0.5, 0.15625, ((1, 8),)),
        "first_bias": scatter_about(splits[2], (FF,), 0.5, 3.0, ((0, 8),), jnp.float32),
        "hidden_grad": draw_hidden_grad(jax.random.fold_in(splits[7], 71), 0),
        "other_squares": jnp.clip(jnp.exp(math.log(1.0) - 2.9957323 * jax.random.uniform(splits[4], (EXAMPLES,), jnp.float32) ** shard_levels(splits[4], (EXAMPLES,), ((0, 64),), -0.2, 0.2)), 0.05, 1.0),
        "weight_noise": scatter_about(splits[5], (D, FF), 16.0, 96.0, ((0, 64), (1, 8)), jnp.float32),
        "bias_noise": scatter_about(splits[6], (FF,), 16.0, 96.0, ((0, 8),), jnp.float32),
    }


def gelu_slope(pre_act):
    normal_cdf = 0.5 * (1.0 + lax.erf(pre_act * 0.7071067811865476))
    normal_pdf = jnp.exp(-0.5 * pre_act * pre_act) * 0.3989422804014327
    return normal_cdf + pre_act * normal_pdf

def reference(layer_input, first_weight, first_bias, hidden_grad, other_squares, weight_noise, bias_noise):
    pre_act = jnp.dot(layer_input, first_weight, preferred_element_type=jnp.float32) + first_bias
    pre_grad = (hidden_grad.astype(jnp.float32) * gelu_slope(pre_act)).astype(jnp.bfloat16)
    group_width = FF // N_MP
    summed = jnp.zeros((TOKENS, D), jnp.float32)
    for group in range(N_MP):
        lower = group * group_width
        partial_value = jnp.dot(pre_grad[:, lower:lower + group_width], first_weight[:, lower:lower + group_width].T, preferred_element_type=jnp.float32)
        partial_value = lax.optimization_barrier(partial_value.astype(jnp.bfloat16))
        summed = summed + partial_value.astype(jnp.float32)
    input_grad = summed.astype(jnp.bfloat16)
    input_blocks = layer_input.reshape(EXAMPLES, SEQ, D)
    grad_blocks = pre_grad.reshape(EXAMPLES, SEQ, FF)

    def square_norm(pieces):
        inputs_one, grads_one = pieces
        per_grad = jnp.dot(inputs_one.T, grads_one, preferred_element_type=jnp.float32)
        bias_one = lax.optimization_barrier(jnp.sum(grads_one.astype(jnp.float32), axis=0))
        return jnp.sum(per_grad * per_grad) + jnp.sum(bias_one * bias_one)
    clip_square = float(SEQ * D * FF)
    squares = lax.map(square_norm, (input_blocks, grad_blocks)) + other_squares * clip_square
    clip_bound = math.sqrt(SEQ * D * FF)
    factor = jnp.minimum(1.0, clip_bound / jnp.sqrt(squares))

    def accumulate(carry, pieces):
        total, bias_accum = carry
        inputs_one, grads_one, scale = pieces
        per_grad = jnp.dot(inputs_one.T, grads_one, preferred_element_type=jnp.float32)
        bias_one = lax.optimization_barrier(jnp.sum(grads_one.astype(jnp.float32), axis=0))
        return ((total + scale * per_grad, bias_accum + scale * bias_one), None)
    start = (jnp.zeros((D, FF), jnp.float32), jnp.zeros((FF,), jnp.float32))
    (total, bias_accum), unused = lax.scan(accumulate, start, (input_blocks, grad_blocks, factor))
    weight_grad = (total + weight_noise) / EXAMPLES
    bias_grad = (bias_accum + bias_noise) / EXAMPLES
    return (input_grad, weight_grad, bias_grad)
```

```python
import math

import jax
import jax.numpy as jnp
from jax import lax
from jax.experimental import pallas as pl
from jax.experimental.pallas import tpu as pltpu
from jax.sharding import PartitionSpec as P

D = 1280
FF = 5120
SEQ = 256
EXAMPLES = 128
NX, NY, NH = 4, 8, 2
NZ, NC = 4, 2
N_MP = NZ * NC
R = D // N_MP
F = FF // N_MP
CA = 384
CB = F - CA
XR = D // NX
YR = XR // NY
CLIP_SQUARE = float(SEQ * D * FF)
CLIP_BOUND = math.sqrt(SEQ * D * FF)
F32 = jnp.float32
BF16 = jnp.bfloat16


def gelu_slope(pre_act):
    normal_cdf = 0.5 * (1.0 + lax.erf(pre_act * 0.7071067811865476))
    normal_pdf = jnp.exp(-0.5 * pre_act * pre_act) * 0.3989422804014327
    return normal_cdf + pre_act * normal_pdf


def rows(start, size, align=16):
    return pl.ds(pl.multiple_of(start, align), size)


def kernel(
    x_hbm, w_hbm, h_hbm, bias_ref, other_ref,
    ig_ref, wg_ref, bg_ref,
    x_in, w, h, xg, acc, g, per, nt, bt,
    bsend, brecv, bown, zsend, zrecv, igacc,
    wa, ra1, ra2, suma, ya, yra,
    wb, rb, sumb, xb, xrb,
    zs, zsnd, zrcv, bx, by, bz,
    lsem, ag_s, ag_f, ag_p, ag_r, nsem, nrem, ss_s, ss_r, zz_s, zz_r,
    a1_s, a1_r, a2_s, a2_r, ya_s, ya_r, b_s, b_r, xb_s, xb_r, h_s, h_r,
    bx_s, bx_r, by_s, by_r, bz_s, bz_r,
):
    d, m = lax.axis_index("dp"), lax.axis_index("mp")
    px, py, ph = d // (NY * NH), (d // NH) % NY, d % NH
    z, c = m // NC, m % NC
    sibling = (d, m + 1 - 2 * c)

    def at_z(other):
        return (d, other * NC + c)

    def at_x(k):
        return (((px + k) % NX * NY + py) * NH + ph, m)

    def at_y(k):
        return ((px * NY + (py + k) % NY) * NH + ph, m)

    half_peer = (d + 1 - 2 * ph, m)

    def send(src, dst, ssem, rsem, device):
        return pltpu.make_async_remote_copy(
            src_ref=src, dst_ref=dst, send_sem=ssem, recv_sem=rsem,
            device_id=device, device_id_type=pl.DeviceIdType.MESH,
        )

    load_x = pltpu.make_async_copy(x_hbm, x_in, lsem.at[0])
    load_w = pltpu.make_async_copy(w_hbm, w, lsem.at[1])
    load_h = pltpu.make_async_copy(h_hbm, h, lsem.at[2])
    load_x.start()
    load_w.start()
    load_h.start()
    barrier = pltpu.get_barrier_semaphore()

    def greet(device):
        pl.semaphore_signal(barrier, inc=1, device_id=device, device_id_type=pl.DeviceIdType.MESH)

    for k in range(1, N_MP):
        greet((d, (m + k) % N_MP))
    for k in range(1, NX):
        greet(at_x(k))
    for k in range(1, NY):
        greet(at_y(k))
    greet(half_peer)

    load_x.wait()
    for e in range(2):
        xg[e, rows(m * R, R, 32), :] = jnp.transpose(
            x_in[e * SEQ : (e + 1) * SEQ, :].astype(F32)
        ).astype(BF16)
    pl.semaphore_wait(barrier, N_MP - 1 + NX - 1 + NY - 1 + 1)

    def slot(e, i):
        return xg.at[e, rows(i * R, R, 32), :]

    def ag_copy(e, i, ssem, device):
        return send(slot(e, i), slot(e, i), ssem, ag_r.at[e * N_MP + i], device)

    first = jnp.where(z == NZ - 1, 3, 1)
    order = (2, first, 4 - first)

    def far(k):
        other = (z + k) % NZ
        return (other - z == 3) | (z - other == 3)

    def ag_start(e):
        for j, k in enumerate(order):
            @pl.when(jnp.logical_not(far(k)))
            def _(j=j, k=k):
                ag_copy(e, m, ag_s.at[e * 4 + j], at_z((z + k) % NZ)).start()
        ag_copy(e, m, ag_s.at[e * 4 + 3], sibling).start()

    inner = (z == 1) | (z == 2)
    relay_to = at_z(jnp.where(z == 2, 3, 0))

    def ag_take(e, j):
        i = (z + order[j]) % NZ * NC + c
        ag_copy(e, i, ag_s.at[0], sibling).wait_recv()
        if j == 0:
            @pl.when(inner)
            def _():
                ag_copy(e, i, ag_p.at[e], relay_to).start()
        ag_copy(e, i, ag_f.at[e * 3 + j], sibling).start()

    def ag_rest(e):
        for k in range(NZ):
            i = (z + k) % NZ * NC + 1 - c
            ag_copy(e, i, ag_s.at[0], sibling).wait_recv()

    def ag_sent(e):
        for j, k in enumerate(order):
            @pl.when(jnp.logical_not(far(k)))
            def _(j=j, k=k):
                ag_copy(e, m, ag_s.at[e * 4 + j], at_z((z + k) % NZ)).wait_send()
        ag_copy(e, m, ag_s.at[e * 4 + 3], sibling).wait_send()
        for j in range(3):
            ag_copy(e, m, ag_f.at[e * 3 + j], sibling).wait_send()

        @pl.when(inner)
        def _():
            ag_copy(e, m, ag_p.at[e], relay_to).wait_send()

    def pre_act(e):
        acc[...] = jnp.broadcast_to(bias_ref[...], (SEQ, F))

        def step(b, carry):
            at = rows(b * 256, 256, 256)
            acc[...] += lax.dot_general(
                xg[e, at, :], w[at, :], (((0,), (0,)), ((), ())), preferred_element_type=F32
            )
            return carry

        lax.fori_loop(0, D // 256, step, 0)

    def slope(e):
        def step(b, total):
            at = rows(b * 32, 32, 32)
            grad = h[rows(e * SEQ + b * 32, 32, 32), :].astype(F32)
            value = (grad * gelu_slope(acc[at, :])).astype(BF16)
            g[e, at, :] = value
            wide = value.astype(F32)
            return total + wide[0:8] + wide[8:16] + wide[16:24] + wide[24:32]

        total = lax.fori_loop(0, SEQ // 32, step, jnp.zeros((8, F), F32))
        row = jnp.sum(total, axis=0, keepdims=True)
        bt[e] = jnp.zeros((8, 128), F32)
        for k in range(F // 128):
            bt[e, k : k + 1, :] = row[:, k * 128 : (k + 1) * 128]

    def weight_terms(e):
        def step(b, total):
            at = rows(b * 256, 256, 256)
            value = jnp.dot(xg[e, at, :], g[e], preferred_element_type=F32)
            per[e, at, :] = value
            return total + jnp.sum((value * value).reshape(32, 8, F), axis=0)

        total = lax.fori_loop(0, D // 256, step, jnp.zeros((8, F), F32))
        tile = bt[e] * bt[e]
        for k in range(F // 128):
            tile = tile + total[:, k * 128 : (k + 1) * 128]
        nt[e, m] = tile

    def norm_copy(e, i, k):
        return send(
            nt.at[e, i], nt.at[e, i], nsem.at[e * N_MP + k], nrem.at[e * N_MP + i],
            (d, (m + k) % N_MP),
        )

    def norm_start(e):
        for k in range(1, N_MP):
            norm_copy(e, m, k).start()

    def norm_wait(e):
        for k in range(1, N_MP):
            norm_copy(e, (m + k) % N_MP, k).wait_recv()

    def back_half(e, core, store):
        def step(k, carry):
            at = rows((k * NC + core) * R, R, 32)
            store(k, lax.dot_general(
                w[at, :], g[e], (((1,), (1,)), ((), ())), preferred_element_type=F32
            ))
            return carry

        lax.fori_loop(0, NZ, step, 0)

    def pair_copy(e):
        return send(bsend.at[e], brecv.at[e], ss_s.at[e], ss_r.at[e], sibling)

    def back(e):
        def store_other(k, value):
            bsend[e, k] = value.astype(BF16)

        def store_own(k, value):
            bown[e, k] = value

        back_half(e, 1 - c, store_other)
        pair_copy(e).start()
        back_half(e, c, store_own)

    def z_copy(e, k):
        other = (z + k) % NZ
        return send(
            zsend.at[e, other], zrecv.at[e, k - 1], zz_s.at[e * 3 + k - 1], zz_r.at[e * 3 + k - 1],
            at_z(other),
        )

    def back_send(e):
        pair_copy(e).wait_recv()
        for k in (2, 1, 3):
            other = (z + k) % NZ
            zsend[e, other] = (bown[e, other] + brecv[e, other].astype(F32)).astype(BF16)
            z_copy(e, k).start()
        igacc[e] = bown[e, z] + brecv[e, z].astype(F32)

    def back_take(e):
        total = igacc[e]
        for k in range(1, NZ):
            z_copy(e, k).wait_recv()
            total = total + zrecv[e, k - 1].astype(F32)
        ig_ref[:, e * SEQ : (e + 1) * SEQ] = total.astype(BF16)

    ag_start(0)
    load_w.wait()
    load_h.wait()
    ag_start(1)
    for j in range(3):
        ag_take(0, j)
    ag_rest(0)
    pre_act(0)
    slope(0)
    ag_take(1, 0)
    weight_terms(0)
    norm_start(0)
    ag_take(1, 1)
    back(0)
    ag_take(1, 2)
    ag_rest(1)
    pre_act(1)
    slope(1)
    weight_terms(1)
    norm_start(1)
    back_send(0)
    back(1)
    norm_wait(0)
    norm_wait(1)

    factors = []
    for e in range(2):
        tile = nt[e, 0]
        for i in range(1, N_MP):
            tile = tile + nt[e, i]
        squares = jnp.full((1, 128), jnp.sum(tile) + other_ref[e] * CLIP_SQUARE, F32)
        factors.append(jnp.minimum(1.0, CLIP_BOUND / jnp.sqrt(squares)))
    f0, f1 = factors
    f0a, f1a = jnp.tile(f0, (1, CA // 128)), jnp.tile(f1, (1, CA // 128))
    f0b, f1b = jnp.tile(f0, (1, CB // 128)), jnp.tile(f1, (1, CB // 128))

    def weighted_a(at):
        return f0a * per[0, at, 0:CA] + f1a * per[1, at, 0:CA]

    def weighted_b(at):
        return f0b * per[0, at, CA:F] + f1b * per[1, at, CA:F]

    def fill_a(k):
        owner = (px + k) % NX
        for half in range(2):
            wa[owner * 2 + half] = weighted_a(rows(owner * XR + half * R, R, 32)).astype(BF16)

    def block_b(owner):
        return jnp.concatenate(
            [weighted_b(rows(i * XR + owner * YR, YR, 8)) for i in range(NX)], axis=0
        )

    def fill_b(k):
        owner = (py + k) % NY
        wb[owner] = block_b(owner).astype(BF16)

    right, left = 1, NX - 1

    def a1_copy(way):
        return send(
            wa.at[(px + 2) % NX * 2 + way], ra1.at[way], a1_s.at[way], a1_r.at[way],
            at_x((right, left)[way]),
        )

    def a2_copy(way, half):
        k = (right, left)[way]
        return send(
            wa.at[(px + k) % NX * 2 + half], ra2.at[way, half], a2_s.at[way * 2 + half],
            a2_r.at[way * 2 + half], at_x(k),
        )

    def b_copy(way, k):
        owner = (py + (k if way == 0 else NY - k)) % NY
        part = (slice(0, 80) if way == 0 else slice(80, 160)) if k == 4 else slice(0, 160)
        return send(
            wb.at[owner, part], rb.at[way, k - 1, part], b_s.at[way * 4 + k - 1],
            b_r.at[way * 4 + k - 1], at_y(1 if way == 0 else NY - 1),
        )

    def b_step(k):
        for way in range(2):
            owner = (py + (k if way == 0 else NY - k)) % NY
            b_copy(way, k + 1).wait_recv()
            part = (slice(0, 80) if way == 0 else slice(80, 160)) if k == 3 else slice(0, 160)
            wb[owner, part] = (
                wb[owner, part].astype(F32) + rb[way, k, part].astype(F32)
            ).astype(BF16)
            b_copy(way, k).start()

    def bx_copy(i, k):
        return send(bx.at[i], bx.at[i], bx_s.at[k], bx_r.at[i], at_x(k))

    def by_copy(i, k):
        return send(by.at[i], by.at[i], by_s.at[k], by_r.at[i], at_y(k))

    def bz_copy(i):
        return send(bz.at[i], bz.at[i], bz_s.at[0], bz_r.at[i], half_peer)

    fill_a(2)
    a1_copy(0).start()
    a1_copy(1).start()
    fill_b(4)
    b_copy(0, 4).start()
    b_copy(1, 4).start()
    bx[px] = f0 * bt[0] + f1 * bt[1]
    for k in range(1, NX):
        bx_copy(px, k).start()
    fill_a(1)
    a2_copy(0, 1).start()
    fill_a(3)
    a2_copy(1, 0).start()
    for k in (3, 5, 2, 6, 1, 7):
        fill_b(k)
    b_step(3)
    back_send(1)
    for way in range(2):
        a1_copy(way).wait_recv()
        at = (px + (right, left)[way]) % NX * 2 + way
        wa[at] = (wa[at].astype(F32) + ra1[way].astype(F32)).astype(BF16)
        a2_copy(way, way).start()
    b_step(2)
    for k in range(1, NX):
        bx_copy((px + k) % NX, k).wait_recv()
    by[py] = (bx[0] + bx[1]) + (bx[2] + bx[3])
    for k in range(1, NY):
        by_copy(py, k).start()

    for way in range(2):
        for half in range(2):
            a2_copy(way, half).wait_recv()
    for half in range(2):
        suma[half * R : (half + 1) * R, :] = (
            weighted_a(rows(px * XR + half * R, R, 32))
            + ra2[0, half].astype(F32)
            + ra2[1, half].astype(F32)
        )

    def pack_a(owner):
        block = suma[rows(owner * YR, YR, 8), :]
        parts = [block[:, k * 128 : (k + 1) * 128] for k in range(CA // 128)]
        return jnp.concatenate(parts + [jnp.zeros((8, 128), F32)], axis=0)

    def ya_copy(k):
        return send(
            ya.at[k - 1], yra.at[k - 1], ya_s.at[k - 1], ya_r.at[k - 1], at_y(k)
        )

    for k in (4, 3, 5, 2, 6, 1, 7):
        ya[k - 1] = pack_a((py + k) % NY).astype(BF16)
        ya_copy(k).start()
    b_step(1)
    for way in range(2):
        b_copy(way, 1).wait_recv()
    sumb[...] = block_b(py) + rb[0, 0].astype(F32) + rb[1, 0].astype(F32)

    def pack_b(owner):
        block = sumb[rows(owner * YR, YR, 8), :]
        return jnp.concatenate([block[:, 0:128], block[:, 128:256]], axis=0)

    def xb_copy(k):
        return send(xb.at[k - 1], xrb.at[k - 1], xb_s.at[k - 1], xb_r.at[k - 1], at_x(k))

    for k in (2, 1, 3):
        xb[k - 1] = pack_b((px + k) % NX).astype(BF16)
        xb_copy(k).start()

    for k in range(1, NY):
        by_copy((py + k) % NY, k).wait_recv()
    total = by[0]
    for i in range(1, NY):
        total = total + by[i]
    bz[ph] = total
    bz_copy(ph).start()

    back_take(0)
    back_take(1)

    total = pack_a(py)
    for k in range(1, NY):
        ya_copy(k).wait_recv()
        total = total + yra[k - 1].astype(F32)
    zs[0:120, :] = total[0:120]
    total = pack_b(px)
    for k in range(1, NX):
        xb_copy(k).wait_recv()
        total = total + xrb[k - 1].astype(F32)
    zs[120:200, :] = total

    def of_half(half):
        return [zs[rows(i * YR + half * 16, 24, 8), :] for i in range(F // 128)]

    zsnd[...] = jnp.concatenate(of_half(1 - ph) + [jnp.zeros((8, 128), F32)], axis=0).astype(BF16)
    half_copy = send(zsnd, zrcv, h_s.at[0], h_r.at[0], half_peer)
    half_copy.start()
    bz_copy(1 - ph).wait_recv()
    bg_ref[...] = bz[0] + bz[1]
    mine = of_half(ph)
    half_copy.wait_recv()
    theirs = zrcv[...].astype(F32)
    for i in range(F // 128):
        wg_ref[:, i * 128 : (i + 1) * 128] = mine[i] + theirs[i * 24 : (i + 1) * 24]

    for e in range(2):
        ag_sent(e)
        for k in range(1, N_MP):
            norm_copy(e, m, k).wait_send()
        pair_copy(e).wait_send()
        for k in range(1, NZ):
            z_copy(e, k).wait_send()
    for way in range(2):
        a1_copy(way).wait_send()
        for half in range(2):
            a2_copy(way, half).wait_send()
        for k in range(1, 5):
            b_copy(way, k).wait_send()
    for k in range(1, NY):
        ya_copy(k).wait_send()
        by_copy(py, k).wait_send()
    for k in range(1, NX):
        xb_copy(k).wait_send()
        bx_copy(px, k).wait_send()
    bz_copy(ph).wait_send()
    half_copy.wait_send()


def fused(layer_input, first_weight, hidden_grad, first_bias, other_squares):
    vmem = pl.BlockSpec(memory_space=pltpu.VMEM)
    anywhere = pl.BlockSpec(memory_space=pl.ANY)
    dma = pltpu.SemaphoreType.DMA

    def buf(shape, dtype=BF16):
        return pltpu.VMEM(shape, dtype)

    return pl.pallas_call(
        kernel,
        out_shape=(
            jax.ShapeDtypeStruct((R, 2 * SEQ), BF16),
            jax.ShapeDtypeStruct((24, F), F32),
            jax.ShapeDtypeStruct((8, 128), F32),
        ),
        in_specs=[anywhere] * 3 + [vmem, pl.BlockSpec(memory_space=pltpu.SMEM)],
        out_specs=(vmem, vmem, vmem),
        scratch_shapes=[
            buf((2 * SEQ, R)), buf((D, F)), buf((2 * SEQ, F)),
            buf((2, D, SEQ)), buf((SEQ, F), F32), buf((2, SEQ, F)),
            buf((2, D, F), F32), buf((2, N_MP, 8, 128), F32), buf((2, 8, 128), F32),
            buf((2, NZ, R, SEQ)), buf((2, NZ, R, SEQ)), buf((2, NZ, R, SEQ), F32),
            buf((2, NZ, R, SEQ)), buf((2, NZ - 1, R, SEQ)), buf((2, R, SEQ), F32),
            buf((8, R, CA)), buf((2, R, CA)), buf((2, 2, R, CA)),
            buf((XR, CA), F32), buf((NY - 1, 128, 128)), buf((NY - 1, 128, 128)),
            buf((NY, 160, CB)), buf((2, 4, 160, CB)), buf((160, CB), F32),
            buf((NX - 1, 80, 128)), buf((NX - 1, 80, 128)),
            buf((200, 128), F32), buf((128, 128)), buf((128, 128)),
            buf((NX, 8, 128), F32), buf((NY, 8, 128), F32), buf((NH, 8, 128), F32),
            dma((3,)), dma((8,)), dma((6,)), dma((2,)), dma((16,)),
            dma((16,)), dma((16,)), dma((2,)), dma((2,)), dma((6,)), dma((6,)),
            dma((2,)), dma((2,)), dma((4,)), dma((4,)), dma((7,)), dma((7,)),
            dma((8,)), dma((8,)), dma((3,)), dma((3,)), dma((1,)), dma((1,)),
            dma((NX,)), dma((NX,)), dma((NY,)), dma((NY,)), dma((1,)), dma((NH,)),
        ],
        compiler_params=pltpu.CompilerParams(
            collective_id=0, has_side_effects=True, vmem_limit_bytes=40 * 2**20
        ),
        cost_estimate=pl.CostEstimate(
            flops=6 * 512 * D * F, bytes_accessed=3 * 2**20, transcendentals=2 * 512 * F
        ),
    )(layer_input, first_weight, hidden_grad, first_bias.reshape(1, F), other_squares)


def per_device(
    layer_input, first_weight, first_bias, hidden_grad, other_squares, weight_noise, bias_noise
):
    input_t, weight_sum, bias_sum = fused(
        layer_input, first_weight, hidden_grad, first_bias, other_squares
    )
    half = lax.axis_index("dp") % NH
    mine = lax.dynamic_slice_in_dim(weight_sum, half * 4, weight_noise.shape[0], 0)
    weight_grad = (mine + weight_noise) / EXAMPLES
    bias_grad = (bias_sum[: F // 128].reshape(F) + bias_noise) / EXAMPLES
    return (input_t.T, weight_grad, bias_grad)


def solution(mesh):
    placed = (P("dp", "mp"), P(None, "mp"), P("mp"), P("dp", "mp"), P("dp"), P("dp", "mp"), P("mp"))
    return jax.shard_map(
        per_device,
        mesh=mesh,
        in_specs=placed,
        out_specs=(P("dp", "mp"), P("dp", "mp"), P("mp")),
        check_vma=False,
    )
```

```python
import math

import jax
import jax.numpy as jnp
from jax import lax
from jax.experimental import pallas as pl
from jax.experimental.pallas import tpu as pltpu
from jax.sharding import PartitionSpec as P

D = 1280
FF = 5120
SEQ = 256
EXAMPLES = 128
NX, NY, NH = 4, 8, 2
NZ, NC = 4, 2
N_MP = NZ * NC
R = D // N_MP
F = FF // N_MP
NA = 3
NB = F // 128 - NA
XR = D // NX
YR = XR // NY
CLIP_SQUARE = float(SEQ * D * FF)
CLIP_BOUND = math.sqrt(SEQ * D * FF)
F32 = jnp.float32
BF16 = jnp.bfloat16


def gelu_slope(pre_act):
    normal_cdf = 0.5 * (1.0 + lax.erf(pre_act * 0.7071067811865476))
    normal_pdf = jnp.exp(-0.5 * pre_act * pre_act) * 0.3989422804014327
    return normal_cdf + pre_act * normal_pdf


def rows(start, size, align=16):
    return pl.ds(pl.multiple_of(start, align), size)


def kernel(
    x_hbm, w_hbm, h_hbm, bias_hbm, other_hbm,
    ig_ref, wg_ref, bg_ref,
    w, h, bias, other_ref, xg, acc, g, per, nt, bt,
    bsend, brecv, bown, zsend, zrecv, igacc,
    wa, ra1, ra2, suma, ya, yra,
    wb, rb, sumb, xb, xrb,
    zs, zsnd, zrcv, bx, by, bz,
    lsem, ag_s, ag_f, ag_p, ag_r, nsem, nrem, ss_s, ss_r, zz_s, zz_r,
    a1_s, a1_r, a2_s, a2_r, ya_s, ya_r, b_s, b_r, xb_s, xb_r, h_s, h_r,
    bx_s, bx_r, by_s, by_r, bz_s, bz_r,
):
    d, m = lax.axis_index("dp"), lax.axis_index("mp")
    px, py, ph = d // (NY * NH), (d // NH) % NY, d % NH
    z, c = m // NC, m % NC
    sibling = (d, m + 1 - 2 * c)

    def at_z(other):
        return (d, other * NC + c)

    def at_x(k):
        return (((px + k) % NX * NY + py) * NH + ph, m)

    def at_y(k):
        return ((px * NY + (py + k) % NY) * NH + ph, m)

    half_peer = (d + 1 - 2 * ph, m)

    def send(src, dst, ssem, rsem, device):
        return pltpu.make_async_remote_copy(
            src_ref=src, dst_ref=dst, send_sem=ssem, recv_sem=rsem,
            device_id=device, device_id_type=pl.DeviceIdType.MESH,
        )

    pending = []

    def start(copy, when=None):
        if when is None:
            copy.start()
        else:
            pl.when(when)(copy.start)
        pending.append((copy, when))

    load_x = [
        pltpu.make_async_copy(
            x_hbm.at[:, e * SEQ : (e + 1) * SEQ], xg.at[e, rows(m * R, R, 32), :], lsem.at[e]
        )
        for e in range(2)
    ]
    loads = [
        pltpu.make_async_copy(source, target, lsem.at[2 + i])
        for i, (source, target) in enumerate(
            ((w_hbm, w), (h_hbm, h), (bias_hbm, bias), (other_hbm, other_ref))
        )
    ]
    for load in load_x + loads:
        load.start()
    barrier = pltpu.get_barrier_semaphore()

    def greet(device):
        pl.semaphore_signal(barrier, inc=1, device_id=device, device_id_type=pl.DeviceIdType.MESH)

    for k in range(1, N_MP):
        greet((d, (m + k) % N_MP))
    for k in range(1, NX):
        greet(at_x(k))
    for k in range(1, NY):
        greet(at_y(k))
    greet(half_peer)

    load_x[0].wait()
    load_x[1].wait()
    pl.semaphore_wait(barrier, N_MP - 1 + NX - 1 + NY - 1 + 1)

    def slot(e, i):
        return xg.at[e, rows(i * R, R, 32), :]

    def ag_copy(e, i, ssem, device):
        return send(slot(e, i), slot(e, i), ssem, ag_r.at[e * N_MP + i], device)

    first = jnp.where(z == NZ - 1, 3, 1)
    order = (2, first, 4 - first)

    def far(k):
        other = (z + k) % NZ
        return (other - z == 3) | (z - other == 3)

    def ag_start(e):
        for j, k in enumerate(order):
            start(ag_copy(e, m, ag_s.at[e * 4 + j], at_z((z + k) % NZ)), jnp.logical_not(far(k)))
        start(ag_copy(e, m, ag_s.at[e * 4 + 3], sibling))

    inner = (z == 1) | (z == 2)
    relay_to = at_z(jnp.where(z == 2, 3, 0))

    def ag_take(e, j):
        i = (z + order[j]) % NZ * NC + c
        ag_copy(e, i, ag_s.at[0], sibling).wait_recv()
        if j == 0:
            start(ag_copy(e, i, ag_p.at[e], relay_to), inner)
        start(ag_copy(e, i, ag_f.at[e * 3 + j], sibling))

    def ag_rest(e):
        for k in range(NZ):
            i = (z + k) % NZ * NC + 1 - c
            ag_copy(e, i, ag_s.at[0], sibling).wait_recv()

    def pre_act(e):
        acc[...] = lax.dot_general(
            xg[e], w[...], (((0,), (0,)), ((), ())), preferred_element_type=F32
        ) + bias[...].reshape(1, F)

    def slope(e):
        def step(b, total):
            at = rows(b * 32, 32, 32)
            grad = h[rows(e * SEQ + b * 32, 32, 32), :].astype(F32)
            value = (grad * gelu_slope(acc[at, :])).astype(BF16)
            g[e, at, :] = value
            wide = value.astype(F32)
            return total + wide[0:8] + wide[8:16] + wide[16:24] + wide[24:32]

        total = lax.fori_loop(0, SEQ // 32, step, jnp.zeros((8, F), F32))
        row = jnp.sum(total, axis=0, keepdims=True)
        bt[e] = jnp.zeros((8, 128), F32)
        for k in range(F // 128):
            bt[e, k : k + 1, :] = row[:, k * 128 : (k + 1) * 128]

    def weight_terms(e):
        total = jnp.zeros((8, F), F32)
        for b in range(D // 256):
            at = slice(b * 256, (b + 1) * 256)
            value = jnp.dot(xg[e, at, :], g[e], preferred_element_type=F32)
            per[e, at, :] = value
            total = total + jnp.sum((value * value).reshape(32, 8, F), axis=0)
        tile = bt[e] * bt[e]
        for k in range(F // 128):
            tile = tile + total[:, k * 128 : (k + 1) * 128]
        nt[e, m] = tile

    def norm_copy(e, i, k):
        return send(
            nt.at[e, i], nt.at[e, i], nsem.at[e * N_MP + k], nrem.at[e * N_MP + i],
            (d, (m + k) % N_MP),
        )

    def norm_start(e):
        for k in range(1, N_MP):
            start(norm_copy(e, m, k))

    def norm_wait(e):
        for k in range(1, N_MP):
            norm_copy(e, (m + k) % N_MP, k).wait_recv()

    def back_half(e, core, store):
        for k in range(NZ):
            at = rows((k * NC + core) * R, R, 32)
            store(k, lax.dot_general(
                w[at, :], g[e], (((1,), (1,)), ((), ())), preferred_element_type=F32
            ))

    def pair_copy(e):
        return send(bsend.at[e], brecv.at[e], ss_s.at[e], ss_r.at[e], sibling)

    def back(e):
        def store_other(k, value):
            bsend[e, k] = value.astype(BF16)

        def store_own(k, value):
            bown[e, k] = value

        back_half(e, 1 - c, store_other)
        start(pair_copy(e))
        back_half(e, c, store_own)

    def z_copy(e, k):
        other = (z + k) % NZ
        return send(
            zsend.at[e, other], zrecv.at[e, k - 1], zz_s.at[e * 3 + k - 1], zz_r.at[e * 3 + k - 1],
            at_z(other),
        )

    def back_send(e):
        pair_copy(e).wait_recv()
        for k in (2, 1, 3):
            other = (z + k) % NZ
            zsend[e, other] = (bown[e, other] + brecv[e, other].astype(F32)).astype(BF16)
            start(z_copy(e, k))
        igacc[e] = bown[e, z] + brecv[e, z].astype(F32)

    def back_take(e):
        total = igacc[e]
        for k in range(1, NZ):
            z_copy(e, k).wait_recv()
            total = total + zrecv[e, k - 1].astype(F32)
        ig_ref[:, e * SEQ : (e + 1) * SEQ] = total.astype(BF16)

    ag_start(0)
    ag_start(1)
    for load in loads:
        load.wait()
    for j in range(3):
        ag_take(0, j)
    ag_rest(0)
    pre_act(0)
    slope(0)
    ag_take(1, 0)
    weight_terms(0)
    norm_start(0)
    ag_take(1, 1)
    back(0)
    ag_take(1, 2)
    ag_rest(1)
    pre_act(1)
    slope(1)
    weight_terms(1)
    norm_start(1)
    back_send(0)
    back(1)
    norm_wait(0)
    norm_wait(1)

    factors = []
    for e in range(2):
        tile = nt[e, 0]
        for i in range(1, N_MP):
            tile = tile + nt[e, i]
        squares = jnp.full((1, 128), jnp.sum(tile) + other_ref[e] * CLIP_SQUARE, F32)
        factors.append(jnp.minimum(1.0, CLIP_BOUND / jnp.sqrt(squares)))
    f0, f1 = factors

    def weighted(tile, start, size, align=32):
        at, columns = rows(start, size, align), slice(tile * 128, (tile + 1) * 128)
        return f0 * per[0, at, columns] + f1 * per[1, at, columns]

    def weighted_a(t, i):
        return weighted(t, i * R, R)

    def weighted_b(t, owner):
        return jnp.concatenate(
            [weighted(NA + t, i * XR + owner * YR, YR, 8) for i in range(NX)], axis=0
        )

    step_x = (1, NX - 1)
    step_y = (1, NY - 1)

    def index_a(k, half):
        return (px + k) % NX * 2 + half

    def index_b(way, k):
        return (py + (k if way == 0 else NY - k)) % NY

    def a1_copy(t, way):
        return send(
            wa.at[t, index_a(2, way)], ra1.at[t, way], a1_s.at[t * 2 + way], a1_r.at[t * 2 + way],
            at_x(step_x[way]),
        )

    def a2_copy(t, way, half):
        n = (t * 2 + way) * 2 + half
        return send(
            wa.at[t, index_a(step_x[way], half)], ra2.at[t, way, half], a2_s.at[n], a2_r.at[n],
            at_x(step_x[way]),
        )

    def part_b(way, k):
        return (slice(0, 80), slice(80, 160))[way] if k == 4 else slice(0, 160)

    def b_copy(t, way, k):
        n, part = (t * 2 + way) * 4 + k - 1, part_b(way, k)
        return send(
            wb.at[t, index_b(way, k), part], rb.at[t, way, k - 1, part], b_s.at[n], b_r.at[n],
            at_y(step_y[way]),
        )

    def b_step(t, k):
        for way in range(2):
            owner = index_b(way, k)
            b_copy(t, way, k + 1).wait_recv()
            part = part_b(way, k + 1)
            wb[t, owner, part] = (
                wb[t, owner, part].astype(F32) + rb[t, way, k, part].astype(F32)
            ).astype(BF16)
            start(b_copy(t, way, k))

    def bx_copy(i, k):
        return send(bx.at[i], bx.at[i], bx_s.at[k], bx_r.at[i], at_x(k))

    def by_copy(i, k):
        return send(by.at[i], by.at[i], by_s.at[k], by_r.at[i], at_y(k))

    def bz_copy(i):
        return send(bz.at[i], bz.at[i], bz_s.at[0], bz_r.at[i], half_peer)

    def a2_own(t):
        for way in range(2):
            i = index_a(step_x[way], 1 - way)
            wa[t, i] = weighted_a(t, i).astype(BF16)
            start(a2_copy(t, way, 1 - way))

    def a2_sum(t):
        for way in range(2):
            i = index_a(step_x[way], way)
            value = weighted_a(t, i)
            a1_copy(t, way).wait_recv()
            wa[t, i] = (value + ra1[t, way].astype(F32)).astype(BF16)
            start(a2_copy(t, way, way))

    def ya_copy(t, k):
        n = t * (NY - 1) + k - 1
        return send(ya.at[t, k - 1], yra.at[t, k - 1], ya_s.at[n], ya_r.at[n], at_y(k))

    def pad(value, size):
        return jnp.concatenate([value, jnp.zeros((size - value.shape[0], 128), F32)], axis=0)

    def a_turn(t):
        for half in range(2):
            value = weighted_a(t, px * 2 + half)
            for way in range(2):
                a2_copy(t, way, half).wait_recv()
                value = value + ra2[t, way, half].astype(F32)
            suma[t, half * R : (half + 1) * R, :] = value
        for k in (4, 3, 5, 2, 6, 1, 7):
            block = suma[t, rows((py + k) % NY * YR, YR, 8), :]
            ya[t, k - 1] = pad(block, 48).astype(BF16)
            start(ya_copy(t, k))

    def a_take(t):
        total = suma[t, rows(py * YR, YR, 8), :]
        for k in range(1, NY):
            ya_copy(t, k).wait_recv()
            total = total + yra[t, k - 1].astype(F32)[0:YR]
        zs[t * YR : (t + 1) * YR, :] = total

    def xb_copy(k):
        return send(xb.at[k - 1], xrb.at[k - 1], xb_s.at[k - 1], xb_r.at[k - 1], at_x(k))

    def pack_b(owner):
        at = rows(owner * YR, YR, 8)
        return jnp.concatenate([sumb[t, at, :] for t in range(NB)], axis=0)

    for t in range(NA):
        for way in range(2):
            i = index_a(2, way)
            wa[t, i] = weighted_a(t, i).astype(BF16)
            start(a1_copy(t, way))
    for t in range(NB):
        owner = (py + 4) % NY
        wb[t, owner] = weighted_b(t, owner).astype(BF16)
        for way in range(2):
            start(b_copy(t, way, 4))
    a2_own(0)
    bx[px] = f0 * bt[0] + f1 * bt[1]
    for k in range(1, NX):
        start(bx_copy(px, k))
    for k in (3, 5, 2, 6, 1, 7):
        owner = (py + k) % NY
        for t in range(NB):
            wb[t, owner] = weighted_b(t, owner).astype(BF16)
    for t in range(NB):
        b_step(t, 3)
    a2_sum(0)
    a2_own(1)
    a2_sum(1)
    a2_own(2)
    a2_sum(2)
    back_send(1)
    for k in range(1, NX):
        bx_copy((px + k) % NX, k).wait_recv()
    by[py] = (bx[0] + bx[1]) + (bx[2] + bx[3])
    for k in range(1, NY):
        start(by_copy(py, k))
    for t in range(NB):
        b_step(t, 2)
    a_turn(0)
    b_step(0, 1)
    a_turn(1)
    b_step(1, 1)
    a_turn(2)

    for t in range(NB):
        value = weighted_b(t, py)
        for way in range(2):
            b_copy(t, way, 1).wait_recv()
            value = value + rb[t, way, 0].astype(F32)
        sumb[t] = value
    for k in (2, 1, 3):
        xb[k - 1] = pack_b((px + k) % NX).astype(BF16)
        start(xb_copy(k))

    for k in range(1, NY):
        by_copy((py + k) % NY, k).wait_recv()
    total = by[0]
    for i in range(1, NY):
        total = total + by[i]
    bz[ph] = total
    start(bz_copy(ph))

    back_take(0)
    back_take(1)
    a_take(0)
    a_take(1)
    total = pack_b(px)
    for k in range(1, NX):
        xb_copy(k).wait_recv()
        total = total + xrb[k - 1].astype(F32)
    zs[NA * YR :, :] = total
    a_take(2)

    def of_half(half):
        return [zs[rows(i * YR + half * 16, 24, 8), :] for i in range(F // 128)]

    zsnd[...] = pad(jnp.concatenate(of_half(1 - ph), axis=0), 128).astype(BF16)
    half_copy = send(zsnd, zrcv, h_s.at[0], h_r.at[0], half_peer)
    start(half_copy)
    bz_copy(1 - ph).wait_recv()
    bg_ref[...] = bz[0] + bz[1]
    mine = of_half(ph)
    half_copy.wait_recv()
    theirs = zrcv[...].astype(F32)
    for i in range(F // 128):
        wg_ref[:, i * 128 : (i + 1) * 128] = mine[i] + theirs[i * 24 : (i + 1) * 24]

    for copy, when in pending:
        if when is None:
            copy.wait_send()
        else:
            pl.when(when)(copy.wait_send)


def fused(layer_input, first_weight, hidden_grad, first_bias, other_squares):
    vmem = pl.BlockSpec(memory_space=pltpu.VMEM)
    hbm = pl.BlockSpec(memory_space=pltpu.HBM)
    dma = pltpu.SemaphoreType.DMA

    def buf(shape, dtype=BF16):
        return pltpu.VMEM(shape, dtype)

    return pl.pallas_call(
        kernel,
        out_shape=(
            jax.ShapeDtypeStruct((R, 2 * SEQ), BF16),
            jax.ShapeDtypeStruct((24, F), F32),
            jax.ShapeDtypeStruct((8, 128), F32),
        ),
        in_specs=[hbm] * 5,
        out_specs=(vmem, vmem, vmem),
        scratch_shapes=[
            buf((D, F)), buf((2 * SEQ, F)), buf((F,), F32), pltpu.SMEM((2,), F32),
            buf((2, D, SEQ)), buf((SEQ, F), F32), buf((2, SEQ, F)),
            buf((2, D, F), F32), buf((2, N_MP, 8, 128), F32), buf((2, 8, 128), F32),
            buf((2, NZ, R, SEQ)), buf((2, NZ, R, SEQ)), buf((2, NZ, R, SEQ), F32),
            buf((2, NZ, R, SEQ)), buf((2, NZ - 1, R, SEQ)), buf((2, R, SEQ), F32),
            buf((NA, 8, R, 128)), buf((NA, 2, R, 128)), buf((NA, 2, 2, R, 128)),
            buf((NA, XR, 128), F32), buf((NA, NY - 1, 48, 128)), buf((NA, NY - 1, 48, 128)),
            buf((NB, NY, 160, 128)), buf((NB, 2, 4, 160, 128)), buf((NB, 160, 128), F32),
            buf((NX - 1, 80, 128)), buf((NX - 1, 80, 128)),
            buf((200, 128), F32), buf((128, 128)), buf((128, 128)),
            buf((NX, 8, 128), F32), buf((NY, 8, 128), F32), buf((NH, 8, 128), F32),
            dma((6,)), dma((8,)), dma((6,)), dma((2,)), dma((16,)),
            dma((16,)), dma((16,)), dma((2,)), dma((2,)), dma((6,)), dma((6,)),
            dma((NA * 2,)), dma((NA * 2,)), dma((NA * 4,)), dma((NA * 4,)),
            dma((NA * 7,)), dma((NA * 7,)),
            dma((NB * 8,)), dma((NB * 8,)), dma((3,)), dma((3,)), dma((1,)), dma((1,)),
            dma((NX,)), dma((NX,)), dma((NY,)), dma((NY,)), dma((1,)), dma((NH,)),
        ],
        compiler_params=pltpu.CompilerParams(
            collective_id=0, has_side_effects=True, vmem_limit_bytes=60 * 2**20
        ),
        cost_estimate=pl.CostEstimate(
            flops=6 * 512 * D * F, bytes_accessed=3 * 2**20, transcendentals=2 * 512 * F
        ),
    )(layer_input.T, first_weight, hidden_grad, first_bias, other_squares)


def per_device(
    layer_input, first_weight, first_bias, hidden_grad, other_squares, weight_noise, bias_noise
):
    input_t, weight_sum, bias_sum = fused(
        layer_input, first_weight, hidden_grad, first_bias, other_squares
    )
    half = lax.axis_index("dp") % NH
    mine = lax.dynamic_slice_in_dim(weight_sum, half * 4, weight_noise.shape[0], 0)
    weight_grad = (mine + weight_noise) / EXAMPLES
    bias_grad = (bias_sum[: F // 128].reshape(F) + bias_noise) / EXAMPLES
    return (input_t.T, weight_grad, bias_grad)


def solution(mesh):
    placed = (P("dp", "mp"), P(None, "mp"), P("mp"), P("dp", "mp"), P("dp"), P("dp", "mp"), P("mp"))
    return jax.shard_map(
        per_device,
        mesh=mesh,
        in_specs=placed,
        out_specs=(P("dp", "mp"), P("dp", "mp"), P("mp")),
        check_vma=False,
    )
```

```python
import math

import jax
import jax.numpy as jnp
from jax import lax
from jax.experimental import pallas as pl
from jax.experimental.pallas import tpu as pltpu
from jax.sharding import PartitionSpec as P

D = 1280
FF = 5120
SEQ = 256
EXAMPLES = 128
NX, NY, NH = 4, 8, 2
NZ, NC = 4, 2
N_MP = NZ * NC
R = D // N_MP
F = FF // N_MP
NA = 3
NB = F // 128 - NA
XR = D // NX
YR = XR // NY
CLIP_SQUARE = float(SEQ * D * FF)
CLIP_BOUND = math.sqrt(SEQ * D * FF)
F32 = jnp.float32
BF16 = jnp.bfloat16


def gelu_slope(pre_act):
    normal_cdf = 0.5 * (1.0 + lax.erf(pre_act * 0.7071067811865476))
    normal_pdf = jnp.exp(-0.5 * pre_act * pre_act) * 0.3989422804014327
    return normal_cdf + pre_act * normal_pdf


def rows(start, size, align=16):
    return pl.ds(pl.multiple_of(start, align), size)


def kernel(
    x_hbm, w_hbm, h_hbm, bias_hbm, other_hbm,
    ig_ref, wg_ref, bg_ref,
    w, h, bias, other_ref, xg, acc, g, per, nt, bt,
    bsend, brecv, bown, zsend, zrecv, zrel, igacc,
    wa, ra1, ra2, suma, ya, yra, za, zra, sumz,
    wb, rb, sumb, xb, xrb,
    zs, zsnd, zrcv, bx, by, bz,
    lsem, ag_s, ag_f, ag_p, ag_r, nsem, nrem, ss_s, ss_r, zz_s, zz_r, zl_s, zl_r,
    a1_s, a1_r, a2_s, a2_r, ya_s, ya_r, za_s, za_r, b_s, b_r, xb_s, xb_r, h_s, h_r,
    bx_s, bx_r, by_s, by_r, bz_s, bz_r,
):
    d, m = lax.axis_index("dp"), lax.axis_index("mp")
    px, py, ph = d // (NY * NH), (d // NH) % NY, d % NH
    z, c = m // NC, m % NC
    sibling = (d, m + 1 - 2 * c)

    def at_z(other):
        return (d, other * NC + c)

    def at_x(k):
        return (((px + k) % NX * NY + py) * NH + ph, m)

    def at_y(k):
        return ((px * NY + (py + k) % NY) * NH + ph, m)

    half_peer = (d + 1 - 2 * ph, m)

    def send(src, dst, ssem, rsem, device):
        return pltpu.make_async_remote_copy(
            src_ref=src, dst_ref=dst, send_sem=ssem, recv_sem=rsem,
            device_id=device, device_id_type=pl.DeviceIdType.MESH,
        )

    pending = []

    def start(copy, when=None):
        if when is None:
            copy.start()
        else:
            pl.when(when)(copy.start)
        pending.append((copy, when))

    load_x = [
        pltpu.make_async_copy(
            x_hbm.at[:, e * SEQ : (e + 1) * SEQ], xg.at[e, rows(m * R, R, 32), :], lsem.at[e]
        )
        for e in range(2)
    ]
    loads = [
        pltpu.make_async_copy(source, target, lsem.at[2 + i])
        for i, (source, target) in enumerate(
            ((w_hbm, w), (h_hbm, h), (bias_hbm, bias), (other_hbm, other_ref))
        )
    ]
    for load in load_x + loads:
        load.start()
    barrier = pltpu.get_barrier_semaphore()

    def greet(device):
        pl.semaphore_signal(barrier, inc=1, device_id=device, device_id_type=pl.DeviceIdType.MESH)

    for k in range(1, N_MP):
        greet((d, (m + k) % N_MP))
    for k in range(1, NX):
        greet(at_x(k))
    for k in range(1, NY):
        greet(at_y(k))
    greet(half_peer)

    load_x[0].wait()
    load_x[1].wait()
    pl.semaphore_wait(barrier, N_MP - 1 + NX - 1 + NY - 1 + 1)

    def slot(e, i):
        return xg.at[e, rows(i * R, R, 32), :]

    def ag_copy(e, i, ssem, device):
        return send(slot(e, i), slot(e, i), ssem, ag_r.at[e * N_MP + i], device)

    first = jnp.where(z == NZ - 1, 3, 1)
    order = (2, first, 4 - first)

    def far(k):
        other = (z + k) % NZ
        return (other - z == 3) | (z - other == 3)

    def ag_start(e):
        for j, k in enumerate(order):
            start(ag_copy(e, m, ag_s.at[e * 4 + j], at_z((z + k) % NZ)), jnp.logical_not(far(k)))
        start(ag_copy(e, m, ag_s.at[e * 4 + 3], sibling))

    inner = (z == 1) | (z == 2)
    relay_to = at_z(jnp.where(z == 2, 3, 0))

    def ag_take(e, j):
        i = (z + order[j]) % NZ * NC + c
        ag_copy(e, i, ag_s.at[0], sibling).wait_recv()
        if j == 0:
            start(ag_copy(e, i, ag_p.at[e], relay_to), inner)
        start(ag_copy(e, i, ag_f.at[e * 3 + j], sibling))

    def ag_pair(e, k):
        i = (z + k) % NZ * NC + 1 - c
        ag_copy(e, i, ag_s.at[0], sibling).wait_recv()

    def pre_act(e):
        acc[...] = lax.dot_general(
            xg[e], w[...], (((0,), (0,)), ((), ())), preferred_element_type=F32
        ) + bias[...].reshape(1, F)

    def pre_act_chip(e, k, start_with):
        at = rows((z + k) % NZ * (NC * R), NC * R, 64)
        acc[...] = start_with + lax.dot_general(
            xg[e, at, :], w[at, :], (((0,), (0,)), ((), ())), preferred_element_type=F32
        )

    def slope(e):
        def step(b, total):
            at = rows(b * 32, 32, 32)
            grad = h[rows(e * SEQ + b * 32, 32, 32), :].astype(F32)
            value = (grad * gelu_slope(acc[at, :])).astype(BF16)
            g[e, at, :] = value
            wide = value.astype(F32)
            return total + wide[0:8] + wide[8:16] + wide[16:24] + wide[24:32]

        total = lax.fori_loop(0, SEQ // 32, step, jnp.zeros((8, F), F32))
        row = jnp.sum(total, axis=0, keepdims=True)
        bt[e] = jnp.zeros((8, 128), F32)
        for k in range(F // 128):
            bt[e, k : k + 1, :] = row[:, k * 128 : (k + 1) * 128]

    def weight_terms(e):
        total = jnp.zeros((8, F), F32)
        for b in range(D // 256):
            at = slice(b * 256, (b + 1) * 256)
            value = jnp.dot(xg[e, at, :], g[e], preferred_element_type=F32)
            per[e, at, :] = value
            total = total + jnp.sum((value * value).reshape(32, 8, F), axis=0)
        tile = bt[e] * bt[e]
        for k in range(F // 128):
            tile = tile + total[:, k * 128 : (k + 1) * 128]
        nt[e, m] = tile

    def norm_copy(e, i, k):
        return send(
            nt.at[e, i], nt.at[e, i], nsem.at[e * N_MP + k], nrem.at[e * N_MP + i],
            (d, (m + k) % N_MP),
        )

    def norm_start(e):
        for k in range(1, N_MP):
            start(norm_copy(e, m, k))

    def norm_wait(e):
        for k in range(1, N_MP):
            norm_copy(e, (m + k) % N_MP, k).wait_recv()

    def back_half(e, core, store):
        for k in range(NZ):
            at = rows((k * NC + core) * R, R, 32)
            store(k, lax.dot_general(
                w[at, :], g[e], (((1,), (1,)), ((), ())), preferred_element_type=F32
            ))

    def pair_copy(e):
        return send(bsend.at[e], brecv.at[e], ss_s.at[e], ss_r.at[e], sibling)

    def back(e):
        def store_other(k, value):
            bsend[e, k] = value.astype(BF16)

        def store_own(k, value):
            bown[e, k] = value

        back_half(e, 1 - c, store_other)
        start(pair_copy(e))
        back_half(e, c, store_own)

    def z_copy(e, k):
        other = (z + k) % NZ
        return send(
            zsend.at[e, other], zrecv.at[e, k - 1], zz_s.at[e * 3 + k - 1], zz_r.at[e * 3 + k - 1],
            at_z(other),
        )

    relay = at_z(jnp.where(z == 0, 1, 2))

    def relay_copy(e, other):
        return send(zsend.at[e, other], zrel.at[e], zl_s.at[e], zl_r.at[e], relay)

    def back_send(e):
        pair_copy(e).wait_recv()
        for k in (1, 3, 2):
            other = (z + k) % NZ
            zsend[e, other] = (bown[e, other] + brecv[e, other].astype(F32)).astype(BF16)
            if k == 2:
                start(z_copy(e, k), jnp.logical_not(inner))
            else:
                start(z_copy(e, k), jnp.logical_not(far(k)))
                start(relay_copy(e, other), far(k))
        igacc[e] = bown[e, z] + brecv[e, z].astype(F32)

    def back_relay(e):
        copy = z_copy(e, 2)
        other = (z + 2) % NZ

        @pl.when(inner)
        def _():
            relay_copy(e, other).wait_recv()
            zsend[e, other] = (
                zsend[e, other].astype(F32) + zrel[e].astype(F32)
            ).astype(BF16)

        start(copy, inner)

    def back_take(e):
        for k in range(1, NZ):
            comes = jnp.logical_not((z == NZ - 1) & (k == 3) | (z == 0) & (k == 1))

            @pl.when(comes)
            def _(k=k):
                z_copy(e, k).wait_recv()
                igacc[e] += zrecv[e, k - 1].astype(F32)

        ig_ref[:, e * SEQ : (e + 1) * SEQ] = igacc[e].astype(BF16)

    ag_start(0)
    ag_start(1)
    for load in loads:
        load.wait()
    for j in range(3):
        ag_take(0, j)
    for k in range(NZ):
        ag_pair(0, k)
    pre_act(0)
    slope(0)
    ag_take(1, 0)
    weight_terms(0)
    norm_start(0)
    ag_take(1, 1)
    back(0)
    ag_pair(1, 0)
    pre_act_chip(1, 0, bias[...].reshape(1, F))
    ag_pair(1, order[0])
    pre_act_chip(1, order[0], acc[...])
    ag_take(1, 2)
    ag_pair(1, order[1])
    pre_act_chip(1, order[1], acc[...])
    ag_pair(1, order[2])
    pre_act_chip(1, order[2], acc[...])
    slope(1)
    weight_terms(1)
    norm_start(1)
    back_send(0)
    back(1)
    back_send(1)
    back_relay(0)
    norm_wait(0)
    norm_wait(1)

    factors = []
    for e in range(2):
        tile = nt[e, 0]
        for i in range(1, N_MP):
            tile = tile + nt[e, i]
        squares = jnp.full((1, 128), jnp.sum(tile) + other_ref[e] * CLIP_SQUARE, F32)
        factors.append(jnp.minimum(1.0, CLIP_BOUND / jnp.sqrt(squares)))
    f0, f1 = factors

    def weighted(tile, start, size, align=32):
        at, columns = rows(start, size, align), slice(tile * 128, (tile + 1) * 128)
        return f0 * per[0, at, columns] + f1 * per[1, at, columns]

    def weighted_a(t, i):
        return weighted(t, i * R, R)

    def weighted_b(t, owner):
        return jnp.concatenate(
            [weighted(NA + t, i * XR + owner * YR, YR, 8) for i in range(NX)], axis=0
        )

    step_x = (1, NX - 1)
    step_y = (1, NY - 1)

    def index_a(k, half):
        return (px + k) % NX * 2 + half

    def index_b(way, k):
        return (py + (k if way == 0 else NY - k)) % NY

    def a1_copy(t, way):
        return send(
            wa.at[t, index_a(2, way)], ra1.at[t, way], a1_s.at[t * 2 + way], a1_r.at[t * 2 + way],
            at_x(step_x[way]),
        )

    def a2_copy(t, way, half):
        n = (t * 2 + way) * 2 + half
        return send(
            wa.at[t, index_a(step_x[way], half)], ra2.at[t, way, half], a2_s.at[n], a2_r.at[n],
            at_x(step_x[way]),
        )

    def part_b(way, k):
        return (slice(0, 80), slice(80, 160))[way] if k == 4 else slice(0, 160)

    def b_copy(t, way, k):
        n, part = (t * 2 + way) * 4 + k - 1, part_b(way, k)
        return send(
            wb.at[t, index_b(way, k), part], rb.at[t, way, k - 1, part], b_s.at[n], b_r.at[n],
            at_y(step_y[way]),
        )

    def b_step(t, k):
        for way in range(2):
            owner = index_b(way, k)
            b_copy(t, way, k + 1).wait_recv()
            part = part_b(way, k + 1)
            wb[t, owner, part] = (
                wb[t, owner, part].astype(F32) + rb[t, way, k, part].astype(F32)
            ).astype(BF16)
            start(b_copy(t, way, k))

    def bx_copy(i, k):
        return send(bx.at[i], bx.at[i], bx_s.at[k], bx_r.at[i], at_x(k))

    def by_copy(i, k):
        return send(by.at[i], by.at[i], by_s.at[k], by_r.at[i], at_y(k))

    def bz_copy(i):
        return send(bz.at[i], bz.at[i], bz_s.at[0], bz_r.at[i], half_peer)

    def a2_own(t):
        for way in range(2):
            i = index_a(step_x[way], 1 - way)
            wa[t, i] = weighted_a(t, i).astype(BF16)
            start(a2_copy(t, way, 1 - way))

    def a2_sum(t):
        for way in range(2):
            i = index_a(step_x[way], way)
            value = weighted_a(t, i)
            a1_copy(t, way).wait_recv()
            wa[t, i] = (value + ra1[t, way].astype(F32)).astype(BF16)
            start(a2_copy(t, way, way))

    def ya_copy(t, k):
        n = t * (NY - 1) + k - 1
        return send(ya.at[t, k - 1], yra.at[t, k - 1], ya_s.at[n], ya_r.at[n], at_y(k))

    def pad(value, size):
        return jnp.concatenate([value, jnp.zeros((size - value.shape[0], 128), F32)], axis=0)

    def za_copy(t):
        return send(za.at[t], zra.at[t], za_s.at[t], za_r.at[t], half_peer)

    def a_turn(t):
        for half in range(2):
            value = weighted_a(t, px * 2 + half)
            for way in range(2):
                a2_copy(t, way, half).wait_recv()
                value = value + ra2[t, way, half].astype(F32)
            suma[t, half * R : (half + 1) * R, :] = value
        za[t] = jnp.concatenate(
            [suma[t, rows(i * YR + (1 - ph) * 16, 24, 8), :] for i in range(NY)], axis=0
        ).astype(BF16)
        start(za_copy(t))

    def a_mid(t):
        za_copy(t).wait_recv()
        theirs = zra[t].astype(F32)
        for i in range(NY):
            sumz[t, i * 24 : (i + 1) * 24, :] = (
                suma[t, rows(i * YR + ph * 16, 24, 8), :] + theirs[i * 24 : (i + 1) * 24]
            )
        for k in (4, 3, 5, 2, 6, 1, 7):
            block = sumz[t, rows((py + k) % NY * 24, 24, 8), :]
            ya[t, k - 1] = pad(block, 32).astype(BF16)
            start(ya_copy(t, k))

    def a_take(t):
        total = sumz[t, rows(py * 24, 24, 8), :]
        for k in range(1, NY):
            ya_copy(t, k).wait_recv()
            total = total + yra[t, k - 1].astype(F32)[0:24]
        wg_ref[:, t * 128 : (t + 1) * 128] = total

    def xb_copy(k):
        return send(xb.at[k - 1], xrb.at[k - 1], xb_s.at[k - 1], xb_r.at[k - 1], at_x(k))

    def pack_b(owner):
        at = rows(owner * YR, YR, 8)
        return jnp.concatenate([sumb[t, at, :] for t in range(NB)], axis=0)

    for t in range(NA):
        for way in range(2):
            i = index_a(2, way)
            wa[t, i] = weighted_a(t, i).astype(BF16)
            start(a1_copy(t, way))
    for t in range(NB):
        owner = (py + 4) % NY
        wb[t, owner] = weighted_b(t, owner).astype(BF16)
        for way in range(2):
            start(b_copy(t, way, 4))
    a2_own(0)
    bx[px] = f0 * bt[0] + f1 * bt[1]
    for k in range(1, NX):
        start(bx_copy(px, k))
    for k in (3, 5, 2, 6, 1, 7):
        owner = (py + k) % NY
        for t in range(NB):
            wb[t, owner] = weighted_b(t, owner).astype(BF16)
    for t in range(NB):
        b_step(t, 3)
    a2_sum(0)
    a2_own(1)
    a2_sum(1)
    a2_own(2)
    a2_sum(2)
    back_relay(1)
    for k in range(1, NX):
        bx_copy((px + k) % NX, k).wait_recv()
    by[py] = (bx[0] + bx[1]) + (bx[2] + bx[3])
    for k in range(1, NY):
        start(by_copy(py, k))
    for t in range(NB):
        b_step(t, 2)
    a_turn(0)
    b_step(0, 1)
    a_turn(1)
    b_step(1, 1)
    a_turn(2)
    a_mid(0)
    for k in range(1, NY):
        by_copy((py + k) % NY, k).wait_recv()
    total = by[0]
    for i in range(1, NY):
        total = total + by[i]
    bz[ph] = total
    start(bz_copy(ph))
    a_mid(1)
    for t in range(NB):
        value = weighted_b(t, py)
        for way in range(2):
            b_copy(t, way, 1).wait_recv()
            value = value + rb[t, way, 0].astype(F32)
        sumb[t] = value
    for k in (2, 1, 3):
        xb[k - 1] = pack_b((px + k) % NX).astype(BF16)
        start(xb_copy(k))
    a_mid(2)
    total = pack_b(px)
    for k in range(1, NX):
        xb_copy(k).wait_recv()
        total = total + xrb[k - 1].astype(F32)
    zs[...] = total

    def of_half(half):
        return [zs[rows(t * YR + half * 16, 24, 8), :] for t in range(NB)]

    zsnd[...] = jnp.concatenate(of_half(1 - ph), axis=0).astype(BF16)
    half_copy = send(zsnd, zrcv, h_s.at[0], h_r.at[0], half_peer)
    start(half_copy)
    back_take(0)
    back_take(1)
    bz_copy(1 - ph).wait_recv()
    bg_ref[...] = bz[0] + bz[1]
    for t in range(NA):
        a_take(t)
    mine = of_half(ph)
    half_copy.wait_recv()
    theirs = zrcv[...].astype(F32)
    for t in range(NB):
        wg_ref[:, (NA + t) * 128 : (NA + t + 1) * 128] = mine[t] + theirs[t * 24 : (t + 1) * 24]

    for copy, when in pending:
        if when is None:
            copy.wait_send()
        else:
            pl.when(when)(copy.wait_send)


def fused(layer_input, first_weight, hidden_grad, first_bias, other_squares):
    vmem = pl.BlockSpec(memory_space=pltpu.VMEM)
    hbm = pl.BlockSpec(memory_space=pltpu.HBM)
    dma = pltpu.SemaphoreType.DMA

    def buf(shape, dtype=BF16):
        return pltpu.VMEM(shape, dtype)

    return pl.pallas_call(
        kernel,
        out_shape=(
            jax.ShapeDtypeStruct((R, 2 * SEQ), BF16),
            jax.ShapeDtypeStruct((24, F), F32),
            jax.ShapeDtypeStruct((8, 128), F32),
        ),
        in_specs=[hbm] * 5,
        out_specs=(vmem, vmem, vmem),
        scratch_shapes=[
            buf((D, F)), buf((2 * SEQ, F)), buf((F,), F32), pltpu.SMEM((2,), F32),
            buf((2, D, SEQ)), buf((SEQ, F), F32), buf((2, SEQ, F)),
            buf((2, D, F), F32), buf((2, N_MP, 8, 128), F32), buf((2, 8, 128), F32),
            buf((2, NZ, R, SEQ)), buf((2, NZ, R, SEQ)), buf((2, NZ, R, SEQ), F32),
            buf((2, NZ, R, SEQ)), buf((2, NZ - 1, R, SEQ)), buf((2, R, SEQ)), buf((2, R, SEQ), F32),
            buf((NA, 8, R, 128)), buf((NA, 2, R, 128)), buf((NA, 2, 2, R, 128)),
            buf((NA, XR, 128), F32), buf((NA, NY - 1, 32, 128)), buf((NA, NY - 1, 32, 128)),
            buf((NA, 192, 128)), buf((NA, 192, 128)), buf((NA, 192, 128), F32),
            buf((NB, NY, 160, 128)), buf((NB, 2, 4, 160, 128)), buf((NB, 160, 128), F32),
            buf((NX - 1, 80, 128)), buf((NX - 1, 80, 128)),
            buf((NB * YR, 128), F32), buf((NB * 24, 128)), buf((NB * 24, 128)),
            buf((NX, 8, 128), F32), buf((NY, 8, 128), F32), buf((NH, 8, 128), F32),
            dma((6,)), dma((8,)), dma((6,)), dma((2,)), dma((16,)),
            dma((16,)), dma((16,)), dma((2,)), dma((2,)), dma((6,)), dma((6,)), dma((2,)), dma((2,)),
            dma((NA * 2,)), dma((NA * 2,)), dma((NA * 4,)), dma((NA * 4,)),
            dma((NA * 7,)), dma((NA * 7,)), dma((NA,)), dma((NA,)),
            dma((NB * 8,)), dma((NB * 8,)), dma((3,)), dma((3,)), dma((1,)), dma((1,)),
            dma((NX,)), dma((NX,)), dma((NY,)), dma((NY,)), dma((1,)), dma((NH,)),
        ],
        compiler_params=pltpu.CompilerParams(
            collective_id=0, has_side_effects=True, vmem_limit_bytes=60 * 2**20
        ),
        cost_estimate=pl.CostEstimate(
            flops=6 * 512 * D * F, bytes_accessed=3 * 2**20, transcendentals=2 * 512 * F
        ),
    )(layer_input.T, first_weight, hidden_grad, first_bias, other_squares)


def per_device(
    layer_input, first_weight, first_bias, hidden_grad, other_squares, weight_noise, bias_noise
):
    input_t, weight_sum, bias_sum = fused(
        layer_input, first_weight, hidden_grad, first_bias, other_squares
    )
    half = lax.axis_index("dp") % NH
    mine = lax.dynamic_slice_in_dim(weight_sum, half * 4, weight_noise.shape[0], 0)
    weight_grad = (mine + weight_noise) / EXAMPLES
    bias_grad = (bias_sum[: F // 128].reshape(F) + bias_noise) / EXAMPLES
    return (input_t.T, weight_grad, bias_grad)


def solution(mesh):
    placed = (P("dp", "mp"), P(None, "mp"), P("mp"), P("dp", "mp"), P("dp"), P("dp", "mp"), P("mp"))
    return jax.shard_map(
        per_device,
        mesh=mesh,
        in_specs=placed,
        out_specs=(P("dp", "mp"), P("dp", "mp"), P("mp")),
        check_vma=False,
    )
```

```python
import math

import jax
import jax.numpy as jnp
from jax import lax
from jax.experimental import pallas as pl
from jax.experimental.pallas import tpu as pltpu
from jax.sharding import PartitionSpec as P

D = 1280
FF = 5120
SEQ = 256
EXAMPLES = 128
NX, NY, NH = 4, 8, 2
NZ, NC = 4, 2
N_MP = NZ * NC
R = D // N_MP
F = FF // N_MP
NA = 3
NB = F // 128 - NA
XR = D // NX
YR = XR // NY
CLIP_SQUARE = float(SEQ * D * FF)
CLIP_BOUND = math.sqrt(SEQ * D * FF)
F32 = jnp.float32
BF16 = jnp.bfloat16


def gelu_slope(pre_act):
    normal_cdf = 0.5 * (1.0 + lax.erf(pre_act * 0.7071067811865476))
    normal_pdf = jnp.exp(-0.5 * pre_act * pre_act) * 0.3989422804014327
    return normal_cdf + pre_act * normal_pdf


def rows(start, size, align=16):
    return pl.ds(pl.multiple_of(start, align), size)


def kernel(
    x_hbm, w_hbm, h_hbm, bias_hbm, other_hbm,
    ig_ref, wg_ref, bg_ref,
    w, h, bias, other_ref, xg, acc, g, per, nt, bt,
    bsend, brecv, bown, zsend, zrecv, igacc,
    wa, ra1, ra2, suma, ya, yra, za, zra, sumz,
    wb, rb, sumb, xb, xrb,
    zs, zsnd, zrcv, bx, by, bz,
    lsem, ag_s, ag_f, ag_p, ag_r, nsem, nrem, ss_s, ss_r, zz_s, zz_r,
    a1_s, a1_r, a2_s, a2_r, ya_s, ya_r, za_s, za_r, b_s, b_r, xb_s, xb_r, h_s, h_r,
    bx_s, bx_r, by_s, by_r, bz_s, bz_r,
):
    d, m = lax.axis_index("dp"), lax.axis_index("mp")
    px, py, ph = d // (NY * NH), (d // NH) % NY, d % NH
    z, c = m // NC, m % NC
    sibling = (d, m + 1 - 2 * c)

    def at_z(other):
        return (d, other * NC + c)

    def at_x(k):
        return (((px + k) % NX * NY + py) * NH + ph, m)

    def at_y(k):
        return ((px * NY + (py + k) % NY) * NH + ph, m)

    half_peer = (d + 1 - 2 * ph, m)

    def send(src, dst, ssem, rsem, device):
        return pltpu.make_async_remote_copy(
            src_ref=src, dst_ref=dst, send_sem=ssem, recv_sem=rsem,
            device_id=device, device_id_type=pl.DeviceIdType.MESH,
        )

    pending = []

    def start(copy, when=None):
        if when is None:
            copy.start()
        else:
            pl.when(when)(copy.start)
        pending.append((copy, when))

    load_x = [
        pltpu.make_async_copy(
            x_hbm.at[:, e * SEQ : (e + 1) * SEQ], xg.at[e, rows(m * R, R, 32), :], lsem.at[e]
        )
        for e in range(2)
    ]
    loads = [
        pltpu.make_async_copy(source, target, lsem.at[2 + i])
        for i, (source, target) in enumerate(
            ((w_hbm, w), (h_hbm, h), (bias_hbm, bias), (other_hbm, other_ref))
        )
    ]
    for load in load_x + loads:
        load.start()
    barrier = pltpu.get_barrier_semaphore()

    def greet(device):
        pl.semaphore_signal(barrier, inc=1, device_id=device, device_id_type=pl.DeviceIdType.MESH)

    for k in range(1, N_MP):
        greet((d, (m + k) % N_MP))
    for k in range(1, NX):
        greet(at_x(k))
    for k in range(1, NY):
        greet(at_y(k))
    greet(half_peer)

    load_x[0].wait()
    load_x[1].wait()
    pl.semaphore_wait(barrier, N_MP - 1 + NX - 1 + NY - 1 + 1)

    def slot(e, i):
        return xg.at[e, rows(i * R, R, 32), :]

    def ag_copy(e, i, ssem, device):
        return send(slot(e, i), slot(e, i), ssem, ag_r.at[e * N_MP + i], device)

    first = jnp.where(z == NZ - 1, 3, 1)
    order = (2, first, 4 - first)

    def far(k):
        other = (z + k) % NZ
        return (other - z == 3) | (z - other == 3)

    def ag_start(e):
        for j, k in enumerate(order):
            start(ag_copy(e, m, ag_s.at[e * 4 + j], at_z((z + k) % NZ)), jnp.logical_not(far(k)))
        start(ag_copy(e, m, ag_s.at[e * 4 + 3], sibling))

    inner = (z == 1) | (z == 2)
    relay_to = at_z(jnp.where(z == 2, 3, 0))

    def ag_take(e, j):
        i = (z + order[j]) % NZ * NC + c
        ag_copy(e, i, ag_s.at[0], sibling).wait_recv()
        if j == 0:
            start(ag_copy(e, i, ag_p.at[e], relay_to), inner)
        start(ag_copy(e, i, ag_f.at[e * 3 + j], sibling))

    def ag_pair(e, k):
        i = (z + k) % NZ * NC + 1 - c
        ag_copy(e, i, ag_s.at[0], sibling).wait_recv()

    def pre_act(e):
        acc[...] = lax.dot_general(
            xg[e], w[...], (((0,), (0,)), ((), ())), preferred_element_type=F32
        ) + bias[...].reshape(1, F)

    def pre_act_chip(e, k, start_with):
        at = rows((z + k) % NZ * (NC * R), NC * R, 64)
        acc[...] = start_with + lax.dot_general(
            xg[e, at, :], w[at, :], (((0,), (0,)), ((), ())), preferred_element_type=F32
        )

    def slope(e):
        def step(b, total):
            at = rows(b * 32, 32, 32)
            grad = h[rows(e * SEQ + b * 32, 32, 32), :].astype(F32)
            value = (grad * gelu_slope(acc[at, :])).astype(BF16)
            g[e, at, :] = value
            wide = value.astype(F32)
            return total + wide[0:8] + wide[8:16] + wide[16:24] + wide[24:32]

        total = lax.fori_loop(0, SEQ // 32, step, jnp.zeros((8, F), F32))
        row = jnp.sum(total, axis=0, keepdims=True)
        bt[e] = jnp.zeros((8, 128), F32)
        for k in range(F // 128):
            bt[e, k : k + 1, :] = row[:, k * 128 : (k + 1) * 128]

    def weight_terms(e):
        total = jnp.zeros((8, F), F32)
        for b in range(D // 256):
            at = slice(b * 256, (b + 1) * 256)
            value = jnp.dot(xg[e, at, :], g[e], preferred_element_type=F32)
            per[e, at, :] = value
            total = total + jnp.sum((value * value).reshape(32, 8, F), axis=0)
        tile = bt[e] * bt[e]
        for k in range(F // 128):
            tile = tile + total[:, k * 128 : (k + 1) * 128]
        nt[e, m] = tile

    def norm_copy(e, i, k):
        return send(
            nt.at[e, i], nt.at[e, i], nsem.at[e * N_MP + k], nrem.at[e * N_MP + i],
            (d, (m + k) % N_MP),
        )

    def norm_start(e):
        for k in range(1, N_MP):
            start(norm_copy(e, m, k))

    def norm_wait(e):
        for k in range(1, N_MP):
            norm_copy(e, (m + k) % N_MP, k).wait_recv()

    def back_half(e, core, store):
        for k in range(NZ):
            at = rows((k * NC + core) * R, R, 32)
            store(k, lax.dot_general(
                w[at, :], g[e], (((1,), (1,)), ((), ())), preferred_element_type=F32
            ))

    def pair_copy(e):
        return send(bsend.at[e], brecv.at[e], ss_s.at[e], ss_r.at[e], sibling)

    def back(e):
        def store_other(k, value):
            bsend[e, k] = value.astype(BF16)

        def store_own(k, value):
            bown[e, k] = value

        back_half(e, 1 - c, store_other)
        start(pair_copy(e))
        back_half(e, c, store_own)

    def z_copy(e, k):
        other = (z + k) % NZ
        return send(
            zsend.at[e, other], zrecv.at[e, k - 1], zz_s.at[e * 3 + k - 1], zz_r.at[e * 3 + k - 1],
            at_z(other),
        )

    def back_send(e):
        pair_copy(e).wait_recv()
        for k in (2, 1, 3):
            other = (z + k) % NZ
            zsend[e, other] = (bown[e, other] + brecv[e, other].astype(F32)).astype(BF16)
            start(z_copy(e, k))
        igacc[e] = bown[e, z] + brecv[e, z].astype(F32)

    def back_take(e):
        for k in range(1, NZ):
            z_copy(e, k).wait_recv()
            igacc[e] += zrecv[e, k - 1].astype(F32)

        ig_ref[:, e * SEQ : (e + 1) * SEQ] = igacc[e].astype(BF16)

    ag_start(0)
    ag_start(1)
    for load in loads:
        load.wait()
    for j in range(3):
        ag_take(0, j)
    for k in range(NZ):
        ag_pair(0, k)
    pre_act(0)
    slope(0)
    ag_take(1, 0)
    weight_terms(0)
    norm_start(0)
    ag_take(1, 1)
    back(0)
    ag_pair(1, 0)
    pre_act_chip(1, 0, bias[...].reshape(1, F))
    ag_pair(1, order[0])
    pre_act_chip(1, order[0], acc[...])
    ag_take(1, 2)
    ag_pair(1, order[1])
    pre_act_chip(1, order[1], acc[...])
    ag_pair(1, order[2])
    pre_act_chip(1, order[2], acc[...])
    slope(1)
    weight_terms(1)
    norm_start(1)
    back_send(0)
    back(1)
    back_send(1)
    norm_wait(0)
    norm_wait(1)

    factors = []
    for e in range(2):
        tile = nt[e, 0]
        for i in range(1, N_MP):
            tile = tile + nt[e, i]
        squares = jnp.full((1, 128), jnp.sum(tile) + other_ref[e] * CLIP_SQUARE, F32)
        factors.append(jnp.minimum(1.0, CLIP_BOUND / jnp.sqrt(squares)))
    f0, f1 = factors

    def weighted(tile, start, size, align=32):
        at, columns = rows(start, size, align), slice(tile * 128, (tile + 1) * 128)
        return f0 * per[0, at, columns] + f1 * per[1, at, columns]

    def weighted_a(t, i):
        return weighted(t, i * R, R)

    def weighted_b(t, owner):
        return jnp.concatenate(
            [weighted(NA + t, i * XR + owner * YR, YR, 8) for i in range(NX)], axis=0
        )

    step_x = (1, NX - 1)
    step_y = (1, NY - 1)

    def index_a(k, half):
        return (px + k) % NX * 2 + half

    def index_b(way, k):
        return (py + (k if way == 0 else NY - k)) % NY

    def a1_copy(t, way):
        return send(
            wa.at[t, index_a(2, way)], ra1.at[t, way], a1_s.at[t * 2 + way], a1_r.at[t * 2 + way],
            at_x(step_x[way]),
        )

    def a2_copy(t, way, half):
        n = (t * 2 + way) * 2 + half
        return send(
            wa.at[t, index_a(step_x[way], half)], ra2.at[t, way, half], a2_s.at[n], a2_r.at[n],
            at_x(step_x[way]),
        )

    def part_b(way, k):
        return (slice(0, 80), slice(80, 160))[way] if k == 4 else slice(0, 160)

    def b_copy(t, way, k):
        n, part = (t * 2 + way) * 4 + k - 1, part_b(way, k)
        return send(
            wb.at[t, index_b(way, k), part], rb.at[t, way, k - 1, part], b_s.at[n], b_r.at[n],
            at_y(step_y[way]),
        )

    def b_step(t, k):
        for way in range(2):
            owner = index_b(way, k)
            b_copy(t, way, k + 1).wait_recv()
            part = part_b(way, k + 1)
            wb[t, owner, part] = (
                wb[t, owner, part].astype(F32) + rb[t, way, k, part].astype(F32)
            ).astype(BF16)
            start(b_copy(t, way, k))

    def bx_copy(i, k):
        return send(bx.at[i], bx.at[i], bx_s.at[k], bx_r.at[i], at_x(k))

    def by_copy(i, k):
        return send(by.at[i], by.at[i], by_s.at[k], by_r.at[i], at_y(k))

    def bz_copy(i):
        return send(bz.at[i], bz.at[i], bz_s.at[0], bz_r.at[i], half_peer)

    def a2_own(t):
        for way in range(2):
            i = index_a(step_x[way], 1 - way)
            wa[t, i] = weighted_a(t, i).astype(BF16)
            start(a2_copy(t, way, 1 - way))

    def a2_sum(t):
        for way in range(2):
            i = index_a(step_x[way], way)
            value = weighted_a(t, i)
            a1_copy(t, way).wait_recv()
            wa[t, i] = (value + ra1[t, way].astype(F32)).astype(BF16)
            start(a2_copy(t, way, way))

    def ya_copy(t, k):
        n = t * (NY - 1) + k - 1
        return send(ya.at[t, k - 1], yra.at[t, k - 1], ya_s.at[n], ya_r.at[n], at_y(k))

    def pad(value, size):
        return jnp.concatenate([value, jnp.zeros((size - value.shape[0], 128), F32)], axis=0)

    def za_copy(t):
        return send(za.at[t], zra.at[t], za_s.at[t], za_r.at[t], half_peer)

    def a_turn(t):
        for half in range(2):
            value = weighted_a(t, px * 2 + half)
            for way in range(2):
                a2_copy(t, way, half).wait_recv()
                value = value + ra2[t, way, half].astype(F32)
            suma[t, half * R : (half + 1) * R, :] = value
        za[t] = jnp.concatenate(
            [suma[t, rows(i * YR + (1 - ph) * 16, 24, 8), :] for i in range(NY)], axis=0
        ).astype(BF16)
        start(za_copy(t))

    def a_mid(t):
        za_copy(t).wait_recv()
        theirs = zra[t].astype(F32)
        for i in range(NY):
            sumz[t, i * 24 : (i + 1) * 24, :] = (
                suma[t, rows(i * YR + ph * 16, 24, 8), :] + theirs[i * 24 : (i + 1) * 24]
            )
        for k in (4, 3, 5, 2, 6, 1, 7):
            block = sumz[t, rows((py + k) % NY * 24, 24, 8), :]
            ya[t, k - 1] = pad(block, 32).astype(BF16)
            start(ya_copy(t, k))

    def a_take(t):
        total = sumz[t, rows(py * 24, 24, 8), :]
        for k in range(1, NY):
            ya_copy(t, k).wait_recv()
            total = total + yra[t, k - 1].astype(F32)[0:24]
        wg_ref[:, t * 128 : (t + 1) * 128] = total

    def xb_copy(k):
        return send(xb.at[k - 1], xrb.at[k - 1], xb_s.at[k - 1], xb_r.at[k - 1], at_x(k))

    def pack_b(owner):
        at = rows(owner * YR, YR, 8)
        return jnp.concatenate([sumb[t, at, :] for t in range(NB)], axis=0)

    for t in range(NA):
        for way in range(2):
            i = index_a(2, way)
            wa[t, i] = weighted_a(t, i).astype(BF16)
            start(a1_copy(t, way))
    for t in range(NB):
        owner = (py + 4) % NY
        wb[t, owner] = weighted_b(t, owner).astype(BF16)
        for way in range(2):
            start(b_copy(t, way, 4))
    a2_own(0)
    bx[px] = f0 * bt[0] + f1 * bt[1]
    for k in range(1, NX):
        start(bx_copy(px, k))
    for k in (3, 5, 2, 6, 1, 7):
        owner = (py + k) % NY
        for t in range(NB):
            wb[t, owner] = weighted_b(t, owner).astype(BF16)
    for t in range(NB):
        b_step(t, 3)
    a2_sum(0)
    a2_own(1)
    a2_sum(1)
    a2_own(2)
    a2_sum(2)
    for k in range(1, NX):
        bx_copy((px + k) % NX, k).wait_recv()
    by[py] = (bx[0] + bx[1]) + (bx[2] + bx[3])
    for k in range(1, NY):
        start(by_copy(py, k))
    for t in range(NB):
        b_step(t, 2)
    a_turn(0)
    b_step(0, 1)
    a_turn(1)
    b_step(1, 1)
    a_turn(2)
    a_mid(0)
    for k in range(1, NY):
        by_copy((py + k) % NY, k).wait_recv()
    total = by[0]
    for i in range(1, NY):
        total = total + by[i]
    bz[ph] = total
    start(bz_copy(ph))
    a_mid(1)
    for t in range(NB):
        value = weighted_b(t, py)
        for way in range(2):
            b_copy(t, way, 1).wait_recv()
            value = value + rb[t, way, 0].astype(F32)
        sumb[t] = value
    for k in (2, 1, 3):
        xb[k - 1] = pack_b((px + k) % NX).astype(BF16)
        start(xb_copy(k))
    a_mid(2)
    total = pack_b(px)
    for k in range(1, NX):
        xb_copy(k).wait_recv()
        total = total + xrb[k - 1].astype(F32)
    zs[...] = total

    def of_half(half):
        return [zs[rows(t * YR + half * 16, 24, 8), :] for t in range(NB)]

    zsnd[...] = jnp.concatenate(of_half(1 - ph), axis=0).astype(BF16)
    half_copy = send(zsnd, zrcv, h_s.at[0], h_r.at[0], half_peer)
    start(half_copy)
    back_take(0)
    back_take(1)
    bz_copy(1 - ph).wait_recv()
    bg_ref[...] = bz[0] + bz[1]
    for t in range(NA):
        a_take(t)
    mine = of_half(ph)
    half_copy.wait_recv()
    theirs = zrcv[...].astype(F32)
    for t in range(NB):
        wg_ref[:, (NA + t) * 128 : (NA + t + 1) * 128] = mine[t] + theirs[t * 24 : (t + 1) * 24]

    for copy, when in pending:
        if when is None:
            copy.wait_send()
        else:
            pl.when(when)(copy.wait_send)


def fused(layer_input, first_weight, hidden_grad, first_bias, other_squares):
    vmem = pl.BlockSpec(memory_space=pltpu.VMEM)
    hbm = pl.BlockSpec(memory_space=pltpu.HBM)
    dma = pltpu.SemaphoreType.DMA

    def buf(shape, dtype=BF16):
        return pltpu.VMEM(shape, dtype)

    return pl.pallas_call(
        kernel,
        out_shape=(
            jax.ShapeDtypeStruct((R, 2 * SEQ), BF16),
            jax.ShapeDtypeStruct((24, F), F32),
            jax.ShapeDtypeStruct((8, 128), F32),
        ),
        in_specs=[hbm] * 5,
        out_specs=(vmem, vmem, vmem),
        scratch_shapes=[
            buf((D, F)), buf((2 * SEQ, F)), buf((F,), F32), pltpu.SMEM((2,), F32),
            buf((2, D, SEQ)), buf((SEQ, F), F32), buf((2, SEQ, F)),
            buf((2, D, F), F32), buf((2, N_MP, 8, 128), F32), buf((2, 8, 128), F32),
            buf((2, NZ, R, SEQ)), buf((2, NZ, R, SEQ)), buf((2, NZ, R, SEQ), F32),
            buf((2, NZ, R, SEQ)), buf((2, NZ - 1, R, SEQ)), buf((2, R, SEQ), F32),
            buf((NA, 8, R, 128)), buf((NA, 2, R, 128)), buf((NA, 2, 2, R, 128)),
            buf((NA, XR, 128), F32), buf((NA, NY - 1, 32, 128)), buf((NA, NY - 1, 32, 128)),
            buf((NA, 192, 128)), buf((NA, 192, 128)), buf((NA, 192, 128), F32),
            buf((NB, NY, 160, 128)), buf((NB, 2, 4, 160, 128)), buf((NB, 160, 128), F32),
            buf((NX - 1, 80, 128)), buf((NX - 1, 80, 128)),
            buf((NB * YR, 128), F32), buf((NB * 24, 128)), buf((NB * 24, 128)),
            buf((NX, 8, 128), F32), buf((NY, 8, 128), F32), buf((NH, 8, 128), F32),
            dma((6,)), dma((8,)), dma((6,)), dma((2,)), dma((16,)),
            dma((16,)), dma((16,)), dma((2,)), dma((2,)), dma((6,)), dma((6,)),
            dma((NA * 2,)), dma((NA * 2,)), dma((NA * 4,)), dma((NA * 4,)),
            dma((NA * 7,)), dma((NA * 7,)), dma((NA,)), dma((NA,)),
            dma((NB * 8,)), dma((NB * 8,)), dma((3,)), dma((3,)), dma((1,)), dma((1,)),
            dma((NX,)), dma((NX,)), dma((NY,)), dma((NY,)), dma((1,)), dma((NH,)),
        ],
        compiler_params=pltpu.CompilerParams(
            collective_id=0, has_side_effects=True, vmem_limit_bytes=60 * 2**20
        ),
        cost_estimate=pl.CostEstimate(
            flops=6 * 512 * D * F, bytes_accessed=3 * 2**20, transcendentals=2 * 512 * F
        ),
    )(layer_input.T, first_weight, hidden_grad, first_bias, other_squares)


def per_device(
    layer_input, first_weight, first_bias, hidden_grad, other_squares, weight_noise, bias_noise
):
    input_t, weight_sum, bias_sum = fused(
        layer_input, first_weight, hidden_grad, first_bias, other_squares
    )
    half = lax.axis_index("dp") % NH
    mine = lax.dynamic_slice_in_dim(weight_sum, half * 4, weight_noise.shape[0], 0)
    weight_grad = (mine + weight_noise) / EXAMPLES
    bias_grad = (bias_sum[: F // 128].reshape(F) + bias_noise) / EXAMPLES
    return (input_t.T, weight_grad, bias_grad)


def solution(mesh):
    placed = (P("dp", "mp"), P(None, "mp"), P("mp"), P("dp", "mp"), P("dp"), P("dp", "mp"), P("mp"))
    return jax.shard_map(
        per_device,
        mesh=mesh,
        in_specs=placed,
        out_specs=(P("dp", "mp"), P("dp", "mp"), P("mp")),
        check_vma=False,
    )
```

```python
import math

import jax
import jax.numpy as jnp
from jax import lax
from jax.experimental import pallas as pl
from jax.experimental.pallas import tpu as pltpu
from jax.sharding import PartitionSpec as P

D = 1280
FF = 5120
SEQ = 256
EXAMPLES = 128
NX, NY, NH = 4, 8, 2
NZ, NC = 4, 2
N_MP = NZ * NC
R = D // N_MP
F = FF // N_MP
NA = 3
NB = F // 128 - NA
XR = D // NX
YR = XR // NY
CLIP_SQUARE = float(SEQ * D * FF)
CLIP_BOUND = math.sqrt(SEQ * D * FF)
F32 = jnp.float32
BF16 = jnp.bfloat16


def gelu_slope(pre_act):
    normal_cdf = 0.5 * (1.0 + lax.erf(pre_act * 0.7071067811865476))
    normal_pdf = jnp.exp(-0.5 * pre_act * pre_act) * 0.3989422804014327
    return normal_cdf + pre_act * normal_pdf


def rows(start, size, align=16):
    return pl.ds(pl.multiple_of(start, align), size)


def kernel(
    x_hbm, w_hbm, h_hbm, bias_hbm, other_hbm,
    ig_ref, wg_ref, bg_ref,
    w, h, bias, other_ref, xg, acc, g, per, nt, bt,
    bsend, brecv, bown, zsend, zrecv, igacc,
    wa, ra1, ra2, ua, ub, rub, fs, frx, fry, suma, ya, yra, za, zra, sumz,
    wb, rb, sumb, xb, xrb,
    bx, by, bz,
    lsem, ag_s, ag_f, ag_p, ag_r, nsem, nrem, ss_s, ss_r, zz_s, zz_r,
    a1_s, a1_r, ub_s, ub_r, fx_s, fx_r, fy_s, fy_r, a2_s, a2_r, ya_s, ya_r, za_s, za_r, b_s, b_r, xb_s, xb_r,
    bx_s, bx_r, by_s, by_r, bz_s, bz_r,
):
    d, m = lax.axis_index("dp"), lax.axis_index("mp")
    px, py, ph = d // (NY * NH), (d // NH) % NY, d % NH
    z, c = m // NC, m % NC
    sibling = (d, m + 1 - 2 * c)

    def at_z(other):
        return (d, other * NC + c)

    def at_x(k):
        return (((px + k) % NX * NY + py) * NH + ph, m)

    def at_y(k):
        return ((px * NY + (py + k) % NY) * NH + ph, m)

    def at_xh(k, other):
        return (((px + k) % NX * NY + py) * NH + (ph + other) % NH, m)

    half_peer = (d + 1 - 2 * ph, m)

    def send(src, dst, ssem, rsem, device):
        return pltpu.make_async_remote_copy(
            src_ref=src, dst_ref=dst, send_sem=ssem, recv_sem=rsem,
            device_id=device, device_id_type=pl.DeviceIdType.MESH,
        )

    pending = []

    def start(copy, when=None):
        if when is None:
            copy.start()
        else:
            pl.when(when)(copy.start)
        pending.append((copy, when))

    load_x = [
        pltpu.make_async_copy(
            x_hbm.at[:, e * SEQ : (e + 1) * SEQ], xg.at[e, rows(m * R, R, 32), :], lsem.at[e]
        )
        for e in range(2)
    ]
    loads = [
        pltpu.make_async_copy(source, target, lsem.at[2 + i])
        for i, (source, target) in enumerate(
            ((w_hbm, w), (h_hbm, h), (bias_hbm, bias), (other_hbm, other_ref))
        )
    ]
    for load in load_x + loads:
        load.start()
    barrier = pltpu.get_barrier_semaphore()

    def greet(device):
        pl.semaphore_signal(barrier, inc=1, device_id=device, device_id_type=pl.DeviceIdType.MESH)

    for k in range(1, N_MP):
        greet((d, (m + k) % N_MP))
    for k in range(1, NX):
        greet(at_x(k))
        greet(at_xh(k, 1))
    for k in range(1, NY):
        greet(at_y(k))
    greet(half_peer)

    load_x[0].wait()
    load_x[1].wait()
    pl.semaphore_wait(barrier, N_MP - 1 + 2 * (NX - 1) + NY - 1 + 1)

    def slot(e, i):
        return xg.at[e, rows(i * R, R, 32), :]

    def ag_copy(e, i, ssem, device):
        return send(slot(e, i), slot(e, i), ssem, ag_r.at[e * N_MP + i], device)

    first = jnp.where(z == NZ - 1, 3, 1)
    order = (2, first, 4 - first)

    def far(k):
        other = (z + k) % NZ
        return (other - z == 3) | (z - other == 3)

    def ag_start(e):
        for j, k in enumerate(order):
            start(ag_copy(e, m, ag_s.at[e * 4 + j], at_z((z + k) % NZ)), jnp.logical_not(far(k)))
        start(ag_copy(e, m, ag_s.at[e * 4 + 3], sibling))

    inner = (z == 1) | (z == 2)
    relay_to = at_z(jnp.where(z == 2, 3, 0))

    def ag_take(e, j):
        i = (z + order[j]) % NZ * NC + c
        ag_copy(e, i, ag_s.at[0], sibling).wait_recv()
        if j == 0:
            start(ag_copy(e, i, ag_p.at[e], relay_to), inner)
        start(ag_copy(e, i, ag_f.at[e * 3 + j], sibling))

    def ag_pair(e, k):
        i = (z + k) % NZ * NC + 1 - c
        ag_copy(e, i, ag_s.at[0], sibling).wait_recv()

    def pre_act(e):
        acc[...] = lax.dot_general(
            xg[e], w[...], (((0,), (0,)), ((), ())), preferred_element_type=F32
        ) + bias[...].reshape(1, F)

    def pre_act_chip(e, k, start_with):
        at = rows((z + k) % NZ * (NC * R), NC * R, 64)
        acc[...] = start_with + lax.dot_general(
            xg[e, at, :], w[at, :], (((0,), (0,)), ((), ())), preferred_element_type=F32
        )

    def slope(e):
        def step(b, total):
            at = rows(b * 32, 32, 32)
            grad = h[rows(e * SEQ + b * 32, 32, 32), :].astype(F32)
            value = (grad * gelu_slope(acc[at, :])).astype(BF16)
            g[e, at, :] = value
            wide = value.astype(F32)
            return total + wide[0:8] + wide[8:16] + wide[16:24] + wide[24:32]

        total = lax.fori_loop(0, SEQ // 32, step, jnp.zeros((8, F), F32))
        row = jnp.sum(total, axis=0, keepdims=True)
        bt[e] = jnp.zeros((8, 128), F32)
        for k in range(F // 128):
            bt[e, k : k + 1, :] = row[:, k * 128 : (k + 1) * 128]

    def weight_terms(e):
        total = jnp.zeros((8, F), F32)
        for b in range(D // 256):
            at = slice(b * 256, (b + 1) * 256)
            value = jnp.dot(xg[e, at, :], g[e], preferred_element_type=F32)
            per[e, at, :] = value
            total = total + jnp.sum((value * value).reshape(32, 8, F), axis=0)
        tile = bt[e] * bt[e]
        for k in range(F // 128):
            tile = tile + total[:, k * 128 : (k + 1) * 128]
        nt[e, m] = tile

    def norm_copy(e, i, k):
        return send(
            nt.at[e, i], nt.at[e, i], nsem.at[e * N_MP + k], nrem.at[e * N_MP + i],
            (d, (m + k) % N_MP),
        )

    def norm_start(e):
        for k in range(1, N_MP):
            start(norm_copy(e, m, k))

    def norm_wait(e):
        for k in range(1, N_MP):
            norm_copy(e, (m + k) % N_MP, k).wait_recv()

    def back_half(e, core, store):
        for k in range(NZ):
            at = rows((k * NC + core) * R, R, 32)
            store(k, lax.dot_general(
                w[at, :], g[e], (((1,), (1,)), ((), ())), preferred_element_type=F32
            ))

    def pair_copy(e):
        return send(bsend.at[e], brecv.at[e], ss_s.at[e], ss_r.at[e], sibling)

    def back(e):
        def store_other(k, value):
            bsend[e, k] = value.astype(BF16)

        def store_own(k, value):
            bown[e, k] = value

        back_half(e, 1 - c, store_other)
        start(pair_copy(e))
        back_half(e, c, store_own)

    def z_copy(e, k):
        other = (z + k) % NZ
        return send(
            zsend.at[e, other], zrecv.at[e, k - 1], zz_s.at[e * 3 + k - 1], zz_r.at[e * 3 + k - 1],
            at_z(other),
        )

    def back_send(e):
        pair_copy(e).wait_recv()
        for k in (2, 1, 3):
            other = (z + k) % NZ
            zsend[e, other] = (bown[e, other] + brecv[e, other].astype(F32)).astype(BF16)
            start(z_copy(e, k))
        igacc[e] = bown[e, z] + brecv[e, z].astype(F32)

    def back_take(e):
        for k in range(1, NZ):
            z_copy(e, k).wait_recv()
            igacc[e] += zrecv[e, k - 1].astype(F32)

        ig_ref[:, e * SEQ : (e + 1) * SEQ] = igacc[e].astype(BF16)

    step_x = (1, NX - 1)
    step_y = (1, NY - 1)

    def index_a(k, half):
        return (px + k) % NX * 2 + half

    def index_b(way, k):
        return (py + (k if way == 0 else NY - k)) % NY

    def ua_copy(t, way, e):
        n = (t * 2 + way) * 2 + e
        return send(
            ua.at[t, way, e], ra1.at[t, way, e], a1_s.at[n], a1_r.at[n], at_x(step_x[way])
        )

    def ub_copy(t, way, e):
        n = (t * 2 + way) * 2 + e
        return send(
            ub.at[t, way, e], rub.at[t, way, e], ub_s.at[n], ub_r.at[n], at_y(step_y[way])
        )

    def early(e):
        for t in range(NA):
            for way in range(2):
                at = rows(index_a(2, way) * R, R, 32)
                ua[t, way, e] = per[e, at, t * 128 : (t + 1) * 128].astype(BF16)
                start(ua_copy(t, way, e))
        owner = (py + 4) % NY
        for t in range(NB):
            columns = slice((NA + t) * 128, (NA + t + 1) * 128)
            for way in range(2):
                ub[t, way, e] = jnp.concatenate(
                    [
                        per[e, rows(i * XR + owner * YR, YR, 8), columns]
                        for i in (2 * way, 2 * way + 1)
                    ],
                    axis=0,
                ).astype(BF16)
                start(ub_copy(t, way, e))

    ag_start(0)
    ag_start(1)
    for load in loads:
        load.wait()
    for j in range(3):
        ag_take(0, j)
    for k in range(NZ):
        ag_pair(0, k)
    pre_act(0)
    slope(0)
    ag_take(1, 0)
    weight_terms(0)
    norm_start(0)
    early(0)
    ag_take(1, 1)
    back(0)
    ag_pair(1, 0)
    pre_act_chip(1, 0, bias[...].reshape(1, F))
    ag_pair(1, order[0])
    pre_act_chip(1, order[0], acc[...])
    ag_take(1, 2)
    ag_pair(1, order[1])
    pre_act_chip(1, order[1], acc[...])
    ag_pair(1, order[2])
    pre_act_chip(1, order[2], acc[...])
    slope(1)
    weight_terms(1)
    norm_start(1)
    early(1)
    back_send(0)
    back(1)
    back_send(1)
    norm_wait(0)
    norm_wait(1)

    factors = []
    for e in range(2):
        tile = nt[e, 0]
        for i in range(1, N_MP):
            tile = tile + nt[e, i]
        squares = jnp.full((1, 128), jnp.sum(tile) + other_ref[e] * CLIP_SQUARE, F32)
        factors.append(jnp.minimum(1.0, CLIP_BOUND / jnp.sqrt(squares)))
    f0, f1 = factors

    def weighted(tile, start, size, align=32):
        at, columns = rows(start, size, align), slice(tile * 128, (tile + 1) * 128)
        return f0 * per[0, at, columns] + f1 * per[1, at, columns]

    def weighted_a(t, i):
        return weighted(t, i * R, R)

    def weighted_b(t, owner):
        return jnp.concatenate(
            [weighted(NA + t, i * XR + owner * YR, YR, 8) for i in range(NX)], axis=0
        )

    def a2_copy(t, way, half):
        n = (t * 2 + way) * 2 + half
        return send(
            wa.at[t, index_a(step_x[way], half)], ra2.at[t, way, half], a2_s.at[n], a2_r.at[n],
            at_x(step_x[way]),
        )

    def b_copy(t, way, k):
        n, owner = (t * 2 + way) * 3 + k - 1, index_b(way, k)
        return send(
            wb.at[t, owner], rb.at[t, way, k - 1], b_s.at[n], b_r.at[n], at_y(step_y[way])
        )

    def fx_copy(way):
        return send(fs, frx.at[way], fx_s.at[way], fx_r.at[way], at_x(step_x[way]))

    def fy_copy(way):
        return send(fs, fry.at[way], fy_s.at[way], fy_r.at[way], at_y(step_y[way]))

    def scaled(factor, first_part, second_part):
        return (
            factor[0:1] * first_part.astype(F32) + factor[1:2] * second_part.astype(F32)
        )

    def b_step(t, k):
        for way in range(2):
            owner = index_b(way, k)
            value = weighted_b(t, owner)
            if k == 3:
                for e in range(2):
                    ub_copy(t, way, e).wait_recv()
                more = scaled(fry[way], rub[t, way, 0], rub[t, way, 1])
                low, high = value[0:80], value[80:160]
                value = jnp.concatenate(
                    [low + more, high] if way == 0 else [low, high + more], axis=0
                )
            else:
                b_copy(t, way, k + 1).wait_recv()
                value = value + rb[t, way, k].astype(F32)
            wb[t, owner] = value.astype(BF16)
            start(b_copy(t, way, k))

    def bx_copy(i, k):
        return send(bx.at[i], bx.at[i], bx_s.at[k], bx_r.at[i], at_x(k))

    def by_copy(i, k):
        return send(by.at[i], by.at[i], by_s.at[k], by_r.at[i], at_y(k))

    def bz_copy(i):
        return send(bz.at[i], bz.at[i], bz_s.at[0], bz_r.at[i], half_peer)

    def a2_own(t):
        for way in range(2):
            i = index_a(step_x[way], 1 - way)
            wa[t, i] = weighted_a(t, i).astype(BF16)
            start(a2_copy(t, way, 1 - way))

    def a2_sum(t):
        for way in range(2):
            i = index_a(step_x[way], way)
            value = weighted_a(t, i)
            for e in range(2):
                ua_copy(t, way, e).wait_recv()
            value = value + scaled(frx[way], ra1[t, way, 0], ra1[t, way, 1])
            wa[t, i] = value.astype(BF16)
            start(a2_copy(t, way, way))

    def ya_copy(t, k):
        n = t * (NY - 1) + k - 1
        return send(ya.at[t, k - 1], yra.at[t, k - 1], ya_s.at[n], ya_r.at[n], at_y(k))

    def pad(value, size):
        return jnp.concatenate([value, jnp.zeros((size - value.shape[0], 128), F32)], axis=0)

    def za_copy(t):
        return send(za.at[t], zra.at[t], za_s.at[t], za_r.at[t], half_peer)

    def a_turn(t):
        for half in range(2):
            value = weighted_a(t, px * 2 + half)
            for way in range(2):
                a2_copy(t, way, half).wait_recv()
                value = value + ra2[t, way, half].astype(F32)
            suma[t, half * R : (half + 1) * R, :] = value
        za[t] = jnp.concatenate(
            [suma[t, rows(i * YR + (1 - ph) * 16, 24, 8), :] for i in range(NY)], axis=0
        ).astype(BF16)
        start(za_copy(t))

    def a_mid(t):
        za_copy(t).wait_recv()
        theirs = zra[t].astype(F32)
        for i in range(NY):
            sumz[t, i * 24 : (i + 1) * 24, :] = (
                suma[t, rows(i * YR + ph * 16, 24, 8), :] + theirs[i * 24 : (i + 1) * 24]
            )
        for k in (4, 3, 5, 2, 6, 1, 7):
            block = sumz[t, rows((py + k) % NY * 24, 24, 8), :]
            ya[t, k - 1] = pad(block, 32).astype(BF16)
            start(ya_copy(t, k))

    def a_take(t):
        total = sumz[t, rows(py * 24, 24, 8), :]
        for k in range(1, NY):
            ya_copy(t, k).wait_recv()
            total = total + yra[t, k - 1].astype(F32)[0:24]
        wg_ref[:, t * 128 : (t + 1) * 128] = total

    others = [(k, j) for k in (2, 1, 3, 0) for j in (1, 0) if (k, j) != (0, 0)]

    def xb_copy(k, j):
        n = k * 2 + j - 1
        return send(xb.at[n], xrb.at[n], xb_s.at[n], xb_r.at[n], at_xh(k, j))

    def pack_b(owner, half):
        at = rows(owner * YR + half * 16, 24, 8)
        return jnp.concatenate([sumb[t, at, :] for t in range(NB)], axis=0)

    fs[...] = jnp.broadcast_to(f0, (8, 128))
    fs[1:2, :] = f1
    for way in range(2):
        start(fy_copy(way))
        start(fx_copy(way))
    for t in range(NA):
        a2_own(t)
    bx[px] = f0 * bt[0] + f1 * bt[1]
    for k in range(1, NX):
        start(bx_copy(px, k))
    for way in range(2):
        fy_copy(way).wait_recv()
    for t in range(NB):
        b_step(t, 3)
    for way in range(2):
        fx_copy(way).wait_recv()
    for t in range(NA):
        a2_sum(t)
    for k in range(1, NX):
        bx_copy((px + k) % NX, k).wait_recv()
    by[py] = (bx[0] + bx[1]) + (bx[2] + bx[3])
    for k in range(1, NY):
        start(by_copy(py, k))
    b_step(0, 2)
    a_turn(0)
    b_step(1, 2)
    a_turn(1)
    a_turn(2)
    b_step(0, 1)
    a_mid(0)
    b_step(1, 1)
    a_mid(1)
    for k in range(1, NY):
        by_copy((py + k) % NY, k).wait_recv()
    total = by[0]
    for i in range(1, NY):
        total = total + by[i]
    bz[ph] = total
    start(bz_copy(ph))
    a_mid(2)
    for t in range(NB):
        value = weighted_b(t, py)
        for way in range(2):
            b_copy(t, way, 1).wait_recv()
            value = value + rb[t, way, 0].astype(F32)
        sumb[t] = value
    for k, j in others:
        xb[k * 2 + j - 1] = pack_b((px + k) % NX, (ph + j) % NH).astype(BF16)
        start(xb_copy(k, j))
    back_take(0)
    back_take(1)
    bz_copy(1 - ph).wait_recv()
    bg_ref[...] = bz[0] + bz[1]
    for t in range(NA):
        a_take(t)
    total = pack_b(px, ph)
    for k, j in others:
        xb_copy(k, j).wait_recv()
        total = total + xrb[k * 2 + j - 1].astype(F32)
    for t in range(NB):
        wg_ref[:, (NA + t) * 128 : (NA + t + 1) * 128] = total[t * 24 : (t + 1) * 24]

    for copy, when in pending:
        if when is None:
            copy.wait_send()
        else:
            pl.when(when)(copy.wait_send)


def fused(layer_input, first_weight, hidden_grad, first_bias, other_squares):
    vmem = pl.BlockSpec(memory_space=pltpu.VMEM)
    hbm = pl.BlockSpec(memory_space=pltpu.HBM)
    dma = pltpu.SemaphoreType.DMA

    def buf(shape, dtype=BF16):
        return pltpu.VMEM(shape, dtype)

    return pl.pallas_call(
        kernel,
        out_shape=(
            jax.ShapeDtypeStruct((R, 2 * SEQ), BF16),
            jax.ShapeDtypeStruct((24, F), F32),
            jax.ShapeDtypeStruct((8, 128), F32),
        ),
        in_specs=[hbm] * 5,
        out_specs=(vmem, vmem, vmem),
        scratch_shapes=[
            buf((D, F)), buf((2 * SEQ, F)), buf((F,), F32), pltpu.SMEM((2,), F32),
            buf((2, D, SEQ)), buf((SEQ, F), F32), buf((2, SEQ, F)),
            buf((2, D, F), F32), buf((2, N_MP, 8, 128), F32), buf((2, 8, 128), F32),
            buf((2, NZ, R, SEQ)), buf((2, NZ, R, SEQ)), buf((2, NZ, R, SEQ), F32),
            buf((2, NZ, R, SEQ)), buf((2, NZ - 1, R, SEQ)), buf((2, R, SEQ), F32),
            buf((NA, 8, R, 128)), buf((NA, 2, 2, R, 128)), buf((NA, 2, 2, R, 128)),
            buf((NA, 2, 2, R, 128)), buf((NB, 2, 2, 80, 128)), buf((NB, 2, 2, 80, 128)),
            buf((8, 128), F32), buf((2, 8, 128), F32), buf((2, 8, 128), F32),
            buf((NA, XR, 128), F32), buf((NA, NY - 1, 32, 128)), buf((NA, NY - 1, 32, 128)),
            buf((NA, 192, 128)), buf((NA, 192, 128)), buf((NA, 192, 128), F32),
            buf((NB, NY, 160, 128)), buf((NB, 2, 3, 160, 128)), buf((NB, 160, 128), F32),
            buf((7, NB * 24, 128)), buf((7, NB * 24, 128)),
            buf((NX, 8, 128), F32), buf((NY, 8, 128), F32), buf((NH, 8, 128), F32),
            dma((6,)), dma((8,)), dma((6,)), dma((2,)), dma((16,)),
            dma((16,)), dma((16,)), dma((2,)), dma((2,)), dma((6,)), dma((6,)),
            dma((NA * 4,)), dma((NA * 4,)), dma((NB * 4,)), dma((NB * 4,)),
            dma((2,)), dma((2,)), dma((2,)), dma((2,)), dma((NA * 4,)), dma((NA * 4,)),
            dma((NA * 7,)), dma((NA * 7,)), dma((NA,)), dma((NA,)),
            dma((NB * 6,)), dma((NB * 6,)), dma((7,)), dma((7,)),
            dma((NX,)), dma((NX,)), dma((NY,)), dma((NY,)), dma((1,)), dma((NH,)),
        ],
        compiler_params=pltpu.CompilerParams(
            collective_id=0, has_side_effects=True, vmem_limit_bytes=60 * 2**20
        ),
        cost_estimate=pl.CostEstimate(
            flops=6 * 512 * D * F, bytes_accessed=3 * 2**20, transcendentals=2 * 512 * F
        ),
    )(layer_input.T, first_weight, hidden_grad, first_bias, other_squares)


def per_device(
    layer_input, first_weight, first_bias, hidden_grad, other_squares, weight_noise, bias_noise
):
    input_t, weight_sum, bias_sum = fused(
        layer_input, first_weight, hidden_grad, first_bias, other_squares
    )
    half = lax.axis_index("dp") % NH
    mine = lax.dynamic_slice_in_dim(weight_sum, half * 4, weight_noise.shape[0], 0)
    weight_grad = (mine + weight_noise) / EXAMPLES
    bias_grad = (bias_sum[: F // 128].reshape(F) + bias_noise) / EXAMPLES
    return (input_t.T, weight_grad, bias_grad)


def solution(mesh):
    placed = (P("dp", "mp"), P(None, "mp"), P("mp"), P("dp", "mp"), P("dp"), P("dp", "mp"), P("mp"))
    return jax.shard_map(
        per_device,
        mesh=mesh,
        in_specs=placed,
        out_specs=(P("dp", "mp"), P("dp", "mp"), P("mp")),
        check_vma=False,
    )
```

```python
import math

import jax
import jax.numpy as jnp
from jax import lax
from jax.experimental import pallas as pl
from jax.experimental.pallas import tpu as pltpu
from jax.sharding import PartitionSpec as P

D = 1280
FF = 5120
SEQ = 256
EXAMPLES = 128
NX, NY, NH = 4, 8, 2
NZ, NC = 4, 2
N_MP = NZ * NC
R = D // N_MP
F = FF // N_MP
NA = 3
NB = F // 128 - NA
XR = D // NX
YR = XR // NY
CLIP_SQUARE = float(SEQ * D * FF)
CLIP_BOUND = math.sqrt(SEQ * D * FF)
F32 = jnp.float32
BF16 = jnp.bfloat16


def gelu_slope(pre_act):
    normal_cdf = 0.5 * (1.0 + lax.erf(pre_act * 0.7071067811865476))
    normal_pdf = jnp.exp(-0.5 * pre_act * pre_act) * 0.3989422804014327
    return normal_cdf + pre_act * normal_pdf


def rows(start, size, align=16):
    return pl.ds(pl.multiple_of(start, align), size)


def kernel(
    x_hbm, w_hbm, h_hbm, bias_hbm, other_hbm,
    ig_ref, wg_ref, bg_ref,
    w, h, bias, other_ref, xg, acc, g, per, nt, bt,
    bsend, brecv, bown, zsend, zrecv, igacc,
    wa, ra1, ra2, ua, ub, rub, fs, frx, fry, suma, ya, yra, za, zra, sumz,
    wb, rb, sumb, xb, xrb,
    bx, by, bz,
    lsem, ag_s, ag_f, ag_p, ag_r, nsem, nrem, ss_s, ss_r, zz_s, zz_r,
    a1_s, a1_r, ub_s, ub_r, fx_s, fx_r, fy_s, fy_r, a2_s, a2_r, ya_s, ya_r, za_s, za_r, b_s, b_r, xb_s, xb_r,
    bx_s, bx_r, by_s, by_r, bz_s, bz_r,
):
    d, m = lax.axis_index("dp"), lax.axis_index("mp")
    px, py, ph = d // (NY * NH), (d // NH) % NY, d % NH
    z, c = m // NC, m % NC
    sibling = (d, m + 1 - 2 * c)

    def at_z(other):
        return (d, other * NC + c)

    def at_x(k):
        return (((px + k) % NX * NY + py) * NH + ph, m)

    def at_y(k):
        return ((px * NY + (py + k) % NY) * NH + ph, m)

    def at_xh(k, other):
        return (((px + k) % NX * NY + py) * NH + (ph + other) % NH, m)

    half_peer = (d + 1 - 2 * ph, m)

    def send(src, dst, ssem, rsem, device):
        return pltpu.make_async_remote_copy(
            src_ref=src, dst_ref=dst, send_sem=ssem, recv_sem=rsem,
            device_id=device, device_id_type=pl.DeviceIdType.MESH,
        )

    pending = []

    def start(copy, when=None):
        if when is None:
            copy.start()
        else:
            pl.when(when)(copy.start)
        pending.append((copy, when))

    load_x = [
        pltpu.make_async_copy(
            x_hbm.at[:, e * SEQ : (e + 1) * SEQ], xg.at[e, rows(m * R, R, 32), :], lsem.at[e]
        )
        for e in range(2)
    ]
    loads = [
        pltpu.make_async_copy(source, target, lsem.at[2 + i])
        for i, (source, target) in enumerate(
            ((w_hbm, w), (h_hbm, h), (bias_hbm, bias), (other_hbm, other_ref))
        )
    ]
    for load in load_x + loads:
        load.start()
    barrier = pltpu.get_barrier_semaphore()

    def greet(device):
        pl.semaphore_signal(barrier, inc=1, device_id=device, device_id_type=pl.DeviceIdType.MESH)

    for k in range(1, N_MP):
        greet((d, (m + k) % N_MP))
    for k in range(1, NX):
        greet(at_x(k))
        greet(at_xh(k, 1))
    for k in range(1, NY):
        greet(at_y(k))
    greet(half_peer)

    load_x[0].wait()
    load_x[1].wait()
    pl.semaphore_wait(barrier, N_MP - 1 + 2 * (NX - 1) + NY - 1 + 1)

    def slot(e, i):
        return xg.at[e, rows(i * R, R, 32), :]

    def ag_copy(e, i, ssem, device):
        return send(slot(e, i), slot(e, i), ssem, ag_r.at[e * N_MP + i], device)

    first = jnp.where(z == NZ - 1, 3, 1)
    order = (2, first, 4 - first)

    def far(k):
        other = (z + k) % NZ
        return (other - z == 3) | (z - other == 3)

    def ag_start(e):
        for j, k in enumerate(order):
            start(ag_copy(e, m, ag_s.at[e * 4 + j], at_z((z + k) % NZ)), jnp.logical_not(far(k)))
        start(ag_copy(e, m, ag_s.at[e * 4 + 3], sibling))

    inner = (z == 1) | (z == 2)
    relay_to = at_z(jnp.where(z == 2, 3, 0))

    def ag_take(e, j):
        i = (z + order[j]) % NZ * NC + c
        ag_copy(e, i, ag_s.at[0], sibling).wait_recv()
        if j == 0:
            start(ag_copy(e, i, ag_p.at[e], relay_to), inner)
        start(ag_copy(e, i, ag_f.at[e * 3 + j], sibling))

    def ag_pair(e, k):
        i = (z + k) % NZ * NC + 1 - c
        ag_copy(e, i, ag_s.at[0], sibling).wait_recv()

    def pre_act(e):
        acc[...] = lax.dot_general(
            xg[e], w[...], (((0,), (0,)), ((), ())), preferred_element_type=F32
        ) + bias[...].reshape(1, F)

    def pre_act_chip(e, k, start_with):
        at = rows((z + k) % NZ * (NC * R), NC * R, 64)
        acc[...] = start_with + lax.dot_general(
            xg[e, at, :], w[at, :], (((0,), (0,)), ((), ())), preferred_element_type=F32
        )

    def slope(e):
        def step(b, total):
            at = rows(b * 32, 32, 32)
            grad = h[rows(e * SEQ + b * 32, 32, 32), :].astype(F32)
            value = (grad * gelu_slope(acc[at, :])).astype(BF16)
            g[e, at, :] = value
            wide = value.astype(F32)
            return total + wide[0:8] + wide[8:16] + wide[16:24] + wide[24:32]

        total = lax.fori_loop(0, SEQ // 32, step, jnp.zeros((8, F), F32))
        row = jnp.sum(total, axis=0, keepdims=True)
        bt[e] = jnp.zeros((8, 128), F32)
        for k in range(F // 128):
            bt[e, k : k + 1, :] = row[:, k * 128 : (k + 1) * 128]

    def weight_terms(e):
        total = jnp.zeros((8, F), F32)
        for b in range(D // 256):
            at = slice(b * 256, (b + 1) * 256)
            value = jnp.dot(xg[e, at, :], g[e], preferred_element_type=F32)
            per[e, at, :] = value
            total = total + jnp.sum((value * value).reshape(32, 8, F), axis=0)
        tile = bt[e] * bt[e]
        for k in range(F // 128):
            tile = tile + total[:, k * 128 : (k + 1) * 128]
        nt[e, m] = tile

    def norm_copy(e, i, k):
        return send(
            nt.at[e, i], nt.at[e, i], nsem.at[e * N_MP + k], nrem.at[e * N_MP + i],
            (d, (m + k) % N_MP),
        )

    def norm_start(e):
        for k in range(1, N_MP):
            start(norm_copy(e, m, k))

    def norm_wait(e):
        for k in range(1, N_MP):
            norm_copy(e, (m + k) % N_MP, k).wait_recv()

    def back_half(e, core, store):
        for k in range(NZ):
            at = rows((k * NC + core) * R, R, 32)
            store(k, lax.dot_general(
                w[at, :], g[e], (((1,), (1,)), ((), ())), preferred_element_type=F32
            ))

    def pair_copy(e):
        return send(bsend.at[e], brecv.at[e], ss_s.at[e], ss_r.at[e], sibling)

    def back(e):
        def store_other(k, value):
            bsend[e, k] = value.astype(BF16)

        def store_own(k, value):
            bown[e, k] = value

        back_half(e, 1 - c, store_other)
        start(pair_copy(e))
        back_half(e, c, store_own)

    def z_copy(e, k):
        other = (z + k) % NZ
        return send(
            zsend.at[e, other], zrecv.at[e, k - 1], zz_s.at[e * 3 + k - 1], zz_r.at[e * 3 + k - 1],
            at_z(other),
        )

    def back_send(e):
        pair_copy(e).wait_recv()
        for k in (2, 1, 3):
            other = (z + k) % NZ
            zsend[e, other] = (bown[e, other] + brecv[e, other].astype(F32)).astype(BF16)
            start(z_copy(e, k))
        igacc[e] = bown[e, z] + brecv[e, z].astype(F32)

    def back_take(e):
        for k in range(1, NZ):
            z_copy(e, k).wait_recv()
            igacc[e] += zrecv[e, k - 1].astype(F32)

        ig_ref[:, e * SEQ : (e + 1) * SEQ] = igacc[e].astype(BF16)

    step_x = (1, NX - 1)
    step_y = (1, NY - 1)

    def index_a(k, half):
        return (px + k) % NX * 2 + half

    def index_b(way, k):
        return (py + (k if way == 0 else NY - k)) % NY

    def ua_copy(t, way, e):
        n = (t * 2 + way) * 2 + e
        return send(
            ua.at[t, way, e], ra1.at[t, way, e], a1_s.at[n], a1_r.at[n], at_x(step_x[way])
        )

    def ub_copy(t, way, e):
        n = (t * 2 + way) * 2 + e
        return send(
            ub.at[t, way, e], rub.at[t, way, e], ub_s.at[n], ub_r.at[n], at_y(step_y[way])
        )

    def early(e):
        for t in range(NA):
            for way in range(2):
                at = rows(index_a(2, way) * R, R, 32)
                ua[t, way, e] = per[e, at, t * 128 : (t + 1) * 128].astype(BF16)
                start(ua_copy(t, way, e))
        owner = (py + 4) % NY
        for t in range(NB):
            columns = slice((NA + t) * 128, (NA + t + 1) * 128)
            for way in range(2):
                ub[t, way, e] = jnp.concatenate(
                    [
                        per[e, rows(i * XR + owner * YR, YR, 8), columns]
                        for i in (2 * way, 2 * way + 1)
                    ],
                    axis=0,
                ).astype(BF16)
                start(ub_copy(t, way, e))

    ag_start(0)
    ag_start(1)
    for load in loads:
        load.wait()
    for j in range(3):
        ag_take(0, j)
    for k in range(NZ):
        ag_pair(0, k)
    pre_act(0)
    slope(0)
    ag_take(1, 0)
    weight_terms(0)
    norm_start(0)
    early(0)
    ag_take(1, 1)
    back(0)
    ag_pair(1, 0)
    pre_act_chip(1, 0, bias[...].reshape(1, F))
    ag_pair(1, order[0])
    pre_act_chip(1, order[0], acc[...])
    ag_take(1, 2)
    ag_pair(1, order[1])
    pre_act_chip(1, order[1], acc[...])
    ag_pair(1, order[2])
    pre_act_chip(1, order[2], acc[...])
    slope(1)
    weight_terms(1)
    norm_start(1)
    early(1)
    back_send(0)
    back(1)
    back_send(1)
    norm_wait(0)
    norm_wait(1)

    factors = []
    for e in range(2):
        tile = nt[e, 0]
        for i in range(1, N_MP):
            tile = tile + nt[e, i]
        squares = jnp.full((1, 128), jnp.sum(tile) + other_ref[e] * CLIP_SQUARE, F32)
        factors.append(jnp.minimum(1.0, CLIP_BOUND / jnp.sqrt(squares)))
    f0, f1 = factors

    def weighted(tile, start, size, align=32):
        at, columns = rows(start, size, align), slice(tile * 128, (tile + 1) * 128)
        return f0 * per[0, at, columns] + f1 * per[1, at, columns]

    def weighted_a(t, i):
        return weighted(t, i * R, R)

    def weighted_b(t, owner):
        return jnp.concatenate(
            [weighted(NA + t, i * XR + owner * YR, YR, 8) for i in range(NX)], axis=0
        )

    def a2_copy(t, way, half):
        n = (t * 2 + way) * 2 + half
        return send(
            wa.at[t, index_a(step_x[way], half)], ra2.at[t, way, half], a2_s.at[n], a2_r.at[n],
            at_x(step_x[way]),
        )

    def b_copy(t, way, k):
        n, owner = (t * 2 + way) * 3 + k - 1, index_b(way, k)
        return send(
            wb.at[t, owner], rb.at[t, way, k - 1], b_s.at[n], b_r.at[n], at_y(step_y[way])
        )

    def fx_copy(way):
        return send(fs, frx.at[way], fx_s.at[way], fx_r.at[way], at_x(step_x[way]))

    def fy_copy(way):
        return send(fs, fry.at[way], fy_s.at[way], fy_r.at[way], at_y(step_y[way]))

    def scaled(factor, first_part, second_part):
        return (
            factor[0:1] * first_part.astype(F32) + factor[1:2] * second_part.astype(F32)
        )

    def b_step(t, k):
        for way in range(2):
            owner = index_b(way, k)
            value = weighted_b(t, owner)
            if k == 3:
                for e in range(2):
                    ub_copy(t, way, e).wait_recv()
                more = scaled(fry[way], rub[t, way, 0], rub[t, way, 1])
                low, high = value[0:80], value[80:160]
                value = jnp.concatenate(
                    [low + more, high] if way == 0 else [low, high + more], axis=0
                )
            else:
                b_copy(t, way, k + 1).wait_recv()
                value = value + rb[t, way, k].astype(F32)
            wb[t, owner] = value.astype(BF16)
            start(b_copy(t, way, k))

    def bx_copy(i, k):
        return send(bx.at[i], bx.at[i], bx_s.at[k], bx_r.at[i], at_x(k))

    def by_copy(i, k):
        return send(by.at[i], by.at[i], by_s.at[k], by_r.at[i], at_y(k))

    def bz_copy(i):
        return send(bz.at[i], bz.at[i], bz_s.at[0], bz_r.at[i], half_peer)

    def a2_own(t):
        for way in range(2):
            i = index_a(step_x[way], 1 - way)
            wa[t, i] = weighted_a(t, i).astype(BF16)
            start(a2_copy(t, way, 1 - way))

    def a2_sum(t):
        for way in range(2):
            i = index_a(step_x[way], way)
            value = weighted_a(t, i)
            for e in range(2):
                ua_copy(t, way, e).wait_recv()
            value = value + scaled(frx[way], ra1[t, way, 0], ra1[t, way, 1])
            wa[t, i] = value.astype(BF16)
            start(a2_copy(t, way, way))

    def ya_copy(t, k):
        n = t * (NY - 1) + k - 1
        return send(ya.at[t, k - 1], yra.at[t, k - 1], ya_s.at[n], ya_r.at[n], at_y(k))

    def pad(value, size):
        return jnp.concatenate([value, jnp.zeros((size - value.shape[0], 128), F32)], axis=0)

    def za_copy(t):
        return send(za.at[t], zra.at[t], za_s.at[t], za_r.at[t], half_peer)

    def a_turn(t):
        for half in range(2):
            value = weighted_a(t, px * 2 + half)
            for way in range(2):
                a2_copy(t, way, half).wait_recv()
                value = value + ra2[t, way, half].astype(F32)
            suma[t, half * R : (half + 1) * R, :] = value
        za[t] = jnp.concatenate(
            [suma[t, rows(i * YR + (1 - ph) * 16, 24, 8), :] for i in range(NY)], axis=0
        ).astype(BF16)
        start(za_copy(t))

    def a_mid(t):
        za_copy(t).wait_recv()
        theirs = zra[t].astype(F32)
        for i in range(NY):
            sumz[t, i * 24 : (i + 1) * 24, :] = (
                suma[t, rows(i * YR + ph * 16, 24, 8), :] + theirs[i * 24 : (i + 1) * 24]
            )
        for k in (4, 3, 5, 2, 6, 1, 7):
            block = sumz[t, rows((py + k) % NY * 24, 24, 8), :]
            ya[t, k - 1] = pad(block, 32).astype(BF16)
            start(ya_copy(t, k))

    def a_take(t):
        total = sumz[t, rows(py * 24, 24, 8), :]
        for k in range(1, NY):
            ya_copy(t, k).wait_recv()
            total = total + yra[t, k - 1].astype(F32)[0:24]
        wg_ref[:, t * 128 : (t + 1) * 128] = total

    others = [(k, j) for k in (2, 1, 3, 0) for j in (1, 0) if (k, j) != (0, 0)]

    def xb_copy(k, j):
        n = k * 2 + j - 1
        return send(xb.at[n], xrb.at[n], xb_s.at[n], xb_r.at[n], at_xh(k, j))

    def pack_b(owner, half):
        at = rows(owner * YR + half * 16, 24, 8)
        return jnp.concatenate([sumb[t, at, :] for t in range(NB)], axis=0)

    fs[...] = jnp.broadcast_to(f0, (8, 128))
    fs[1:2, :] = f1
    for way in range(2):
        start(fy_copy(way))
        start(fx_copy(way))
    for t in range(NA):
        a2_own(t)
    bx[px] = f0 * bt[0] + f1 * bt[1]
    for k in range(1, NX):
        start(bx_copy(px, k))
    for way in range(2):
        fy_copy(way).wait_recv()
    for t in range(NB):
        b_step(t, 3)
    for way in range(2):
        fx_copy(way).wait_recv()
    for t in range(NA):
        a2_sum(t)
    for k in range(1, NX):
        bx_copy((px + k) % NX, k).wait_recv()
    by[py] = (bx[0] + bx[1]) + (bx[2] + bx[3])
    for k in range(1, NY):
        start(by_copy(py, k))
    b_step(0, 2)
    b_step(1, 2)
    a_turn(0)
    a_turn(1)
    a_turn(2)
    b_step(0, 1)
    b_step(1, 1)
    a_mid(0)
    for k in range(1, NY):
        by_copy((py + k) % NY, k).wait_recv()
    total = by[0]
    for i in range(1, NY):
        total = total + by[i]
    bz[ph] = total
    start(bz_copy(ph))
    a_mid(1)
    for t in range(NB):
        value = weighted_b(t, py)
        for way in range(2):
            b_copy(t, way, 1).wait_recv()
            value = value + rb[t, way, 0].astype(F32)
        sumb[t] = value
    for k, j in others:
        xb[k * 2 + j - 1] = pack_b((px + k) % NX, (ph + j) % NH).astype(BF16)
        start(xb_copy(k, j))
    a_mid(2)
    back_take(0)
    back_take(1)
    bz_copy(1 - ph).wait_recv()
    bg_ref[...] = bz[0] + bz[1]
    for t in range(NA):
        a_take(t)
    total = pack_b(px, ph)
    for k, j in others:
        xb_copy(k, j).wait_recv()
        total = total + xrb[k * 2 + j - 1].astype(F32)
    for t in range(NB):
        wg_ref[:, (NA + t) * 128 : (NA + t + 1) * 128] = total[t * 24 : (t + 1) * 24]

    for copy, when in pending:
        if when is None:
            copy.wait_send()
        else:
            pl.when(when)(copy.wait_send)


def fused(layer_input, first_weight, hidden_grad, first_bias, other_squares):
    vmem = pl.BlockSpec(memory_space=pltpu.VMEM)
    hbm = pl.BlockSpec(memory_space=pltpu.HBM)
    dma = pltpu.SemaphoreType.DMA

    def buf(shape, dtype=BF16):
        return pltpu.VMEM(shape, dtype)

    return pl.pallas_call(
        kernel,
        out_shape=(
            jax.ShapeDtypeStruct((R, 2 * SEQ), BF16),
            jax.ShapeDtypeStruct((24, F), F32),
            jax.ShapeDtypeStruct((8, 128), F32),
        ),
        in_specs=[hbm] * 5,
        out_specs=(vmem, vmem, vmem),
        scratch_shapes=[
            buf((D, F)), buf((2 * SEQ, F)), buf((F,), F32), pltpu.SMEM((2,), F32),
            buf((2, D, SEQ)), buf((SEQ, F), F32), buf((2, SEQ, F)),
            buf((2, D, F), F32), buf((2, N_MP, 8, 128), F32), buf((2, 8, 128), F32),
            buf((2, NZ, R, SEQ)), buf((2, NZ, R, SEQ)), buf((2, NZ, R, SEQ), F32),
            buf((2, NZ, R, SEQ)), buf((2, NZ - 1, R, SEQ)), buf((2, R, SEQ), F32),
            buf((NA, 8, R, 128)), buf((NA, 2, 2, R, 128)), buf((NA, 2, 2, R, 128)),
            buf((NA, 2, 2, R, 128)), buf((NB, 2, 2, 80, 128)), buf((NB, 2, 2, 80, 128)),
            buf((8, 128), F32), buf((2, 8, 128), F32), buf((2, 8, 128), F32),
            buf((NA, XR, 128), F32), buf((NA, NY - 1, 32, 128)), buf((NA, NY - 1, 32, 128)),
            buf((NA, 192, 128)), buf((NA, 192, 128)), buf((NA, 192, 128), F32),
            buf((NB, NY, 160, 128)), buf((NB, 2, 3, 160, 128)), buf((NB, 160, 128), F32),
            buf((7, NB * 24, 128)), buf((7, NB * 24, 128)),
            buf((NX, 8, 128), F32), buf((NY, 8, 128), F32), buf((NH, 8, 128), F32),
            dma((6,)), dma((8,)), dma((6,)), dma((2,)), dma((16,)),
            dma((16,)), dma((16,)), dma((2,)), dma((2,)), dma((6,)), dma((6,)),
            dma((NA * 4,)), dma((NA * 4,)), dma((NB * 4,)), dma((NB * 4,)),
            dma((2,)), dma((2,)), dma((2,)), dma((2,)), dma((NA * 4,)), dma((NA * 4,)),
            dma((NA * 7,)), dma((NA * 7,)), dma((NA,)), dma((NA,)),
            dma((NB * 6,)), dma((NB * 6,)), dma((7,)), dma((7,)),
            dma((NX,)), dma((NX,)), dma((NY,)), dma((NY,)), dma((1,)), dma((NH,)),
        ],
        compiler_params=pltpu.CompilerParams(
            collective_id=0, has_side_effects=True, vmem_limit_bytes=60 * 2**20
        ),
        cost_estimate=pl.CostEstimate(
            flops=6 * 512 * D * F, bytes_accessed=3 * 2**20, transcendentals=2 * 512 * F
        ),
    )(layer_input.T, first_weight, hidden_grad, first_bias, other_squares)


def per_device(
    layer_input, first_weight, first_bias, hidden_grad, other_squares, weight_noise, bias_noise
):
    input_t, weight_sum, bias_sum = fused(
        layer_input, first_weight, hidden_grad, first_bias, other_squares
    )
    half = lax.axis_index("dp") % NH
    mine = lax.dynamic_slice_in_dim(weight_sum, half * 4, weight_noise.shape[0], 0)
    weight_grad = (mine + weight_noise) / EXAMPLES
    bias_grad = (bias_sum[: F // 128].reshape(F) + bias_noise) / EXAMPLES
    return (input_t.T, weight_grad, bias_grad)


def solution(mesh):
    placed = (P("dp", "mp"), P(None, "mp"), P("mp"), P("dp", "mp"), P("dp"), P("dp", "mp"), P("mp"))
    return jax.shard_map(
        per_device,
        mesh=mesh,
        in_specs=placed,
        out_specs=(P("dp", "mp"), P("dp", "mp"), P("mp")),
        check_vma=False,
    )
```

```python
import math

import jax
import jax.numpy as jnp
from jax import lax
from jax.experimental import pallas as pl
from jax.experimental.pallas import tpu as pltpu
from jax.sharding import PartitionSpec as P

D = 1280
FF = 5120
SEQ = 256
EXAMPLES = 128
NX, NY, NH = 4, 8, 2
NZ, NC = 4, 2
N_MP = NZ * NC
R = D // N_MP
F = FF // N_MP
NA = 3
NB = F // 128 - NA
XR = D // NX
YR = XR // NY
CLIP_SQUARE = float(SEQ * D * FF)
CLIP_BOUND = math.sqrt(SEQ * D * FF)
F32 = jnp.float32
BF16 = jnp.bfloat16


def gelu_slope(pre_act):
    normal_cdf = 0.5 * (1.0 + lax.erf(pre_act * 0.7071067811865476))
    normal_pdf = jnp.exp(-0.5 * pre_act * pre_act) * 0.3989422804014327
    return normal_cdf + pre_act * normal_pdf


def rows(start, size, align=16):
    return pl.ds(pl.multiple_of(start, align), size)


def kernel(
    x_hbm, w_hbm, h_hbm, bias_hbm, other_hbm,
    ig_ref, wg_ref, bg_ref,
    w, h, bias, other_ref, xg, acc, g, per, nt, bt,
    bsend, brecv, bown, zsend, zrecv, igacc,
    wa, ra1, ra2, ua, ub, rub, fs, frx, fry, suma, ya, yra, za, zra, sumz,
    wb, rb, sumb, xb, xrb,
    bx, by, bz,
    lsem, ag_s, ag_f, ag_p, ag_r, nsem, nrem, ss_s, ss_r, zz_s, zz_r,
    a1_s, a1_r, ub_s, ub_r, fx_s, fx_r, fy_s, fy_r, a2_s, a2_r, ya_s, ya_r, za_s, za_r, b_s, b_r, xb_s, xb_r,
    bx_s, bx_r, by_s, by_r, bz_s, bz_r,
):
    d, m = lax.axis_index("dp"), lax.axis_index("mp")
    px, py, ph = d // (NY * NH), (d // NH) % NY, d % NH
    z, c = m // NC, m % NC
    sibling = (d, m + 1 - 2 * c)

    def at_z(other):
        return (d, other * NC + c)

    def at_x(k):
        return (((px + k) % NX * NY + py) * NH + ph, m)

    def at_y(k):
        return ((px * NY + (py + k) % NY) * NH + ph, m)

    def at_xh(k, other):
        return (((px + k) % NX * NY + py) * NH + (ph + other) % NH, m)

    half_peer = (d + 1 - 2 * ph, m)

    def send(src, dst, ssem, rsem, device):
        return pltpu.make_async_remote_copy(
            src_ref=src, dst_ref=dst, send_sem=ssem, recv_sem=rsem,
            device_id=device, device_id_type=pl.DeviceIdType.MESH,
        )

    pending = []

    def start(copy, when=None):
        if when is None:
            copy.start()
        else:
            pl.when(when)(copy.start)
        pending.append((copy, when))

    load_x = [
        pltpu.make_async_copy(
            x_hbm.at[:, e * SEQ : (e + 1) * SEQ], xg.at[e, rows(m * R, R, 32), :], lsem.at[e]
        )
        for e in range(2)
    ]
    loads = [
        pltpu.make_async_copy(source, target, lsem.at[2 + i])
        for i, (source, target) in enumerate(
            ((w_hbm, w), (h_hbm, h), (bias_hbm, bias), (other_hbm, other_ref))
        )
    ]
    for load in load_x + loads:
        load.start()
    barrier = pltpu.get_barrier_semaphore()

    def greet(device):
        pl.semaphore_signal(barrier, inc=1, device_id=device, device_id_type=pl.DeviceIdType.MESH)

    for k in range(1, N_MP):
        greet((d, (m + k) % N_MP))
    for k in range(1, NX):
        greet(at_x(k))
        greet(at_xh(k, 1))
    for k in range(1, NY):
        greet(at_y(k))
    greet(half_peer)

    load_x[0].wait()
    load_x[1].wait()
    pl.semaphore_wait(barrier, N_MP - 1 + 2 * (NX - 1) + NY - 1 + 1)

    def slot(e, i):
        return xg.at[e, rows(i * R, R, 32), :]

    def ag_copy(e, i, ssem, device):
        return send(slot(e, i), slot(e, i), ssem, ag_r.at[e * N_MP + i], device)

    first = jnp.where(z == NZ - 1, 3, 1)
    order = (2, first, 4 - first)

    def far(k):
        other = (z + k) % NZ
        return (other - z == 3) | (z - other == 3)

    def ag_start(e):
        for j, k in enumerate(order):
            start(ag_copy(e, m, ag_s.at[e * 4 + j], at_z((z + k) % NZ)), jnp.logical_not(far(k)))
        start(ag_copy(e, m, ag_s.at[e * 4 + 3], sibling))

    inner = (z == 1) | (z == 2)
    relay_to = at_z(jnp.where(z == 2, 3, 0))

    def ag_take(e, j):
        i = (z + order[j]) % NZ * NC + c
        ag_copy(e, i, ag_s.at[0], sibling).wait_recv()
        if j == 0:
            start(ag_copy(e, i, ag_p.at[e], relay_to), inner)
        start(ag_copy(e, i, ag_f.at[e * 3 + j], sibling))

    def ag_pair(e, k):
        i = (z + k) % NZ * NC + 1 - c
        ag_copy(e, i, ag_s.at[0], sibling).wait_recv()

    def pre_act(e):
        acc[...] = lax.dot_general(
            xg[e], w[...], (((0,), (0,)), ((), ())), preferred_element_type=F32
        ) + bias[...].reshape(1, F)

    def pre_act_chip(e, k, start_with):
        at = rows((z + k) % NZ * (NC * R), NC * R, 64)
        acc[...] = start_with + lax.dot_general(
            xg[e, at, :], w[at, :], (((0,), (0,)), ((), ())), preferred_element_type=F32
        )

    def slope(e):
        def step(b, total):
            at = rows(b * 32, 32, 32)
            grad = h[rows(e * SEQ + b * 32, 32, 32), :].astype(F32)
            value = (grad * gelu_slope(acc[at, :])).astype(BF16)
            g[e, at, :] = value
            wide = value.astype(F32)
            return total + wide[0:8] + wide[8:16] + wide[16:24] + wide[24:32]

        total = lax.fori_loop(0, SEQ // 32, step, jnp.zeros((8, F), F32))
        row = jnp.sum(total, axis=0, keepdims=True)
        bt[e] = jnp.zeros((8, 128), F32)
        for k in range(F // 128):
            bt[e, k : k + 1, :] = row[:, k * 128 : (k + 1) * 128]

    def weight_terms(e):
        total = jnp.zeros((8, F), F32)
        for b in range(D // 256):
            at = slice(b * 256, (b + 1) * 256)
            value = jnp.dot(xg[e, at, :], g[e], preferred_element_type=F32)
            per[e, at, :] = value
            total = total + jnp.sum((value * value).reshape(32, 8, F), axis=0)
        tile = bt[e] * bt[e]
        for k in range(F // 128):
            tile = tile + total[:, k * 128 : (k + 1) * 128]
        nt[e, m] = tile

    def norm_copy(e, i, k):
        return send(
            nt.at[e, i], nt.at[e, i], nsem.at[e * N_MP + k], nrem.at[e * N_MP + i],
            (d, (m + k) % N_MP),
        )

    def norm_start(e):
        for k in range(1, N_MP):
            start(norm_copy(e, m, k))

    def norm_wait(e):
        for k in range(1, N_MP):
            norm_copy(e, (m + k) % N_MP, k).wait_recv()

    def back_half(e, core, store):
        for k in range(NZ):
            at = rows((k * NC + core) * R, R, 32)
            store(k, lax.dot_general(
                w[at, :], g[e], (((1,), (1,)), ((), ())), preferred_element_type=F32
            ))

    def pair_copy(e):
        return send(bsend.at[e], brecv.at[e], ss_s.at[e], ss_r.at[e], sibling)

    def back(e):
        def store_other(k, value):
            bsend[e, k] = value.astype(BF16)

        def store_own(k, value):
            bown[e, k] = value

        back_half(e, 1 - c, store_other)
        start(pair_copy(e))
        back_half(e, c, store_own)

    def z_copy(e, k):
        other = (z + k) % NZ
        return send(
            zsend.at[e, other], zrecv.at[e, k - 1], zz_s.at[e * 3 + k - 1], zz_r.at[e * 3 + k - 1],
            at_z(other),
        )

    def back_send(e):
        pair_copy(e).wait_recv()
        for k in (2, 1, 3):
            other = (z + k) % NZ
            zsend[e, other] = (bown[e, other] + brecv[e, other].astype(F32)).astype(BF16)
            start(z_copy(e, k))
        igacc[e] = bown[e, z] + brecv[e, z].astype(F32)

    def back_take(e):
        for k in range(1, NZ):
            z_copy(e, k).wait_recv()
            igacc[e] += zrecv[e, k - 1].astype(F32)

        ig_ref[:, e * SEQ : (e + 1) * SEQ] = igacc[e].astype(BF16)

    step_x = (1, NX - 1)
    step_y = (1, NY - 1)

    def index_a(k, half):
        return (px + k) % NX * 2 + half

    def index_b(way, k):
        return (py + (k if way == 0 else NY - k)) % NY

    def ua_copy(t, way, e):
        n = (t * 2 + way) * 2 + e
        return send(
            ua.at[t, way, e], ra1.at[t, way, e], a1_s.at[n], a1_r.at[n], at_x(step_x[way])
        )

    def ub_copy(t, way, e):
        n = (t * 2 + way) * 2 + e
        return send(
            ub.at[t, way, e], rub.at[t, way, e], ub_s.at[n], ub_r.at[n], at_y(step_y[way])
        )

    def early(e):
        for t in range(NA):
            for way in range(2):
                at = rows(index_a(2, way) * R, R, 32)
                ua[t, way, e] = per[e, at, t * 128 : (t + 1) * 128].astype(BF16)
                start(ua_copy(t, way, e))
        owner = (py + 4) % NY
        for t in range(NB):
            columns = slice((NA + t) * 128, (NA + t + 1) * 128)
            for way in range(2):
                ub[t, way, e] = jnp.concatenate(
                    [
                        per[e, rows(i * XR + owner * YR, YR, 8), columns]
                        for i in (2 * way, 2 * way + 1)
                    ],
                    axis=0,
                ).astype(BF16)
                start(ub_copy(t, way, e))

    ag_start(0)
    ag_start(1)
    for load in loads:
        load.wait()
    for j in range(3):
        ag_take(0, j)
    for k in range(NZ):
        ag_pair(0, k)
    pre_act(0)
    slope(0)
    ag_take(1, 0)
    weight_terms(0)
    norm_start(0)
    early(0)
    ag_take(1, 1)
    back(0)
    ag_pair(1, 0)
    pre_act_chip(1, 0, bias[...].reshape(1, F))
    ag_pair(1, order[0])
    pre_act_chip(1, order[0], acc[...])
    ag_take(1, 2)
    ag_pair(1, order[1])
    pre_act_chip(1, order[1], acc[...])
    ag_pair(1, order[2])
    pre_act_chip(1, order[2], acc[...])
    slope(1)
    weight_terms(1)
    norm_start(1)
    early(1)
    back_send(0)
    back(1)
    norm_wait(0)
    norm_wait(1)

    factors = []
    for e in range(2):
        tile = nt[e, 0]
        for i in range(1, N_MP):
            tile = tile + nt[e, i]
        squares = jnp.full((1, 128), jnp.sum(tile) + other_ref[e] * CLIP_SQUARE, F32)
        factors.append(jnp.minimum(1.0, CLIP_BOUND / jnp.sqrt(squares)))
    f0, f1 = factors

    def weighted(tile, start, size, align=32):
        at, columns = rows(start, size, align), slice(tile * 128, (tile + 1) * 128)
        return f0 * per[0, at, columns] + f1 * per[1, at, columns]

    def weighted_a(t, i):
        return weighted(t, i * R, R)

    def weighted_b(t, owner):
        return jnp.concatenate(
            [weighted(NA + t, i * XR + owner * YR, YR, 8) for i in range(NX)], axis=0
        )

    def a2_copy(t, way, half):
        n = (t * 2 + way) * 2 + half
        return send(
            wa.at[t, index_a(step_x[way], half)], ra2.at[t, way, half], a2_s.at[n], a2_r.at[n],
            at_x(step_x[way]),
        )

    def b_copy(t, way, k):
        n, owner = (t * 2 + way) * 3 + k - 1, index_b(way, k)
        return send(
            wb.at[t, owner], rb.at[t, way, k - 1], b_s.at[n], b_r.at[n], at_y(step_y[way])
        )

    def fx_copy(way):
        return send(fs, frx.at[way], fx_s.at[way], fx_r.at[way], at_x(step_x[way]))

    def fy_copy(way):
        return send(fs, fry.at[way], fy_s.at[way], fy_r.at[way], at_y(step_y[way]))

    def scaled(factor, first_part, second_part):
        return (
            factor[0:1] * first_part.astype(F32) + factor[1:2] * second_part.astype(F32)
        )

    def b_step(t, k):
        for way in range(2):
            owner = index_b(way, k)
            value = weighted_b(t, owner)
            if k == 3:
                for e in range(2):
                    ub_copy(t, way, e).wait_recv()
                more = scaled(fry[way], rub[t, way, 0], rub[t, way, 1])
                low, high = value[0:80], value[80:160]
                value = jnp.concatenate(
                    [low + more, high] if way == 0 else [low, high + more], axis=0
                )
            else:
                b_copy(t, way, k + 1).wait_recv()
                value = value + rb[t, way, k].astype(F32)
            wb[t, owner] = value.astype(BF16)
            start(b_copy(t, way, k))

    def bx_copy(i, k):
        return send(bx.at[i], bx.at[i], bx_s.at[k], bx_r.at[i], at_x(k))

    def by_copy(i, k):
        return send(by.at[i], by.at[i], by_s.at[k], by_r.at[i], at_y(k))

    def bz_copy(i):
        return send(bz.at[i], bz.at[i], bz_s.at[0], bz_r.at[i], half_peer)

    def a2_own(t):
        for way in range(2):
            i = index_a(step_x[way], 1 - way)
            wa[t, i] = weighted_a(t, i).astype(BF16)
            start(a2_copy(t, way, 1 - way))

    def a2_sum(t):
        for way in range(2):
            i = index_a(step_x[way], way)
            value = weighted_a(t, i)
            for e in range(2):
                ua_copy(t, way, e).wait_recv()
            value = value + scaled(frx[way], ra1[t, way, 0], ra1[t, way, 1])
            wa[t, i] = value.astype(BF16)
            start(a2_copy(t, way, way))

    def ya_copy(t, k):
        n = t * (NY - 1) + k - 1
        return send(ya.at[t, k - 1], yra.at[t, k - 1], ya_s.at[n], ya_r.at[n], at_y(k))

    def pad(value, size):
        return jnp.concatenate([value, jnp.zeros((size - value.shape[0], 128), F32)], axis=0)

    def za_copy(t):
        return send(za.at[t], zra.at[t], za_s.at[t], za_r.at[t], half_peer)

    def a_turn(t):
        for half in range(2):
            value = weighted_a(t, px * 2 + half)
            for way in range(2):
                a2_copy(t, way, half).wait_recv()
                value = value + ra2[t, way, half].astype(F32)
            suma[t, half * R : (half + 1) * R, :] = value
        za[t] = jnp.concatenate(
            [suma[t, rows(i * YR + (1 - ph) * 16, 24, 8), :] for i in range(NY)], axis=0
        ).astype(BF16)
        start(za_copy(t))

    def a_mid(t):
        za_copy(t).wait_recv()
        theirs = zra[t].astype(F32)
        for i in range(NY):
            sumz[t, i * 24 : (i + 1) * 24, :] = (
                suma[t, rows(i * YR + ph * 16, 24, 8), :] + theirs[i * 24 : (i + 1) * 24]
            )
        for k in (4, 3, 5, 2, 6, 1, 7):
            block = sumz[t, rows((py + k) % NY * 24, 24, 8), :]
            ya[t, k - 1] = pad(block, 32).astype(BF16)
            start(ya_copy(t, k))

    def a_take(t):
        total = sumz[t, rows(py * 24, 24, 8), :]
        for k in range(1, NY):
            ya_copy(t, k).wait_recv()
            total = total + yra[t, k - 1].astype(F32)[0:24]
        wg_ref[:, t * 128 : (t + 1) * 128] = total

    others = [(k, j) for k in (2, 1, 3, 0) for j in (1, 0) if (k, j) != (0, 0)]

    def xb_copy(k, j):
        n = k * 2 + j - 1
        return send(xb.at[n], xrb.at[n], xb_s.at[n], xb_r.at[n], at_xh(k, j))

    def pack_b(owner, half):
        at = rows(owner * YR + half * 16, 24, 8)
        return jnp.concatenate([sumb[t, at, :] for t in range(NB)], axis=0)

    fs[...] = jnp.broadcast_to(f0, (8, 128))
    fs[1:2, :] = f1
    for way in range(2):
        start(fy_copy(way))
        start(fx_copy(way))
    for t in range(NA):
        a2_own(t)
    bx[px] = f0 * bt[0] + f1 * bt[1]
    for k in range(1, NX):
        start(bx_copy(px, k))
    back_send(1)
    for way in range(2):
        fy_copy(way).wait_recv()
    for t in range(NB):
        b_step(t, 3)
    for way in range(2):
        fx_copy(way).wait_recv()
    for t in range(NA):
        a2_sum(t)
    for k in range(1, NX):
        bx_copy((px + k) % NX, k).wait_recv()
    by[py] = (bx[0] + bx[1]) + (bx[2] + bx[3])
    for k in range(1, NY):
        start(by_copy(py, k))
    b_step(0, 2)
    b_step(1, 2)
    a_turn(0)
    a_turn(1)
    a_turn(2)
    b_step(0, 1)
    b_step(1, 1)
    a_mid(0)
    for k in range(1, NY):
        by_copy((py + k) % NY, k).wait_recv()
    total = by[0]
    for i in range(1, NY):
        total = total + by[i]
    bz[ph] = total
    start(bz_copy(ph))
    a_mid(1)
    for t in range(NB):
        value = weighted_b(t, py)
        for way in range(2):
            b_copy(t, way, 1).wait_recv()
            value = value + rb[t, way, 0].astype(F32)
        sumb[t] = value
    for k, j in others:
        xb[k * 2 + j - 1] = pack_b((px + k) % NX, (ph + j) % NH).astype(BF16)
        start(xb_copy(k, j))
    a_mid(2)
    back_take(0)
    back_take(1)
    bz_copy(1 - ph).wait_recv()
    bg_ref[...] = bz[0] + bz[1]
    for t in range(NA):
        a_take(t)
    total = pack_b(px, ph)
    for k, j in others:
        xb_copy(k, j).wait_recv()
        total = total + xrb[k * 2 + j - 1].astype(F32)
    for t in range(NB):
        wg_ref[:, (NA + t) * 128 : (NA + t + 1) * 128] = total[t * 24 : (t + 1) * 24]

    for copy, when in pending:
        if when is None:
            copy.wait_send()
        else:
            pl.when(when)(copy.wait_send)


def fused(layer_input, first_weight, hidden_grad, first_bias, other_squares):
    vmem = pl.BlockSpec(memory_space=pltpu.VMEM)
    hbm = pl.BlockSpec(memory_space=pltpu.HBM)
    dma = pltpu.SemaphoreType.DMA

    def buf(shape, dtype=BF16):
        return pltpu.VMEM(shape, dtype)

    return pl.pallas_call(
        kernel,
        out_shape=(
            jax.ShapeDtypeStruct((R, 2 * SEQ), BF16),
            jax.ShapeDtypeStruct((24, F), F32),
            jax.ShapeDtypeStruct((8, 128), F32),
        ),
        in_specs=[hbm] * 5,
        out_specs=(vmem, vmem, vmem),
        scratch_shapes=[
            buf((D, F)), buf((2 * SEQ, F)), buf((F,), F32), pltpu.SMEM((2,), F32),
            buf((2, D, SEQ)), buf((SEQ, F), F32), buf((2, SEQ, F)),
            buf((2, D, F), F32), buf((2, N_MP, 8, 128), F32), buf((2, 8, 128), F32),
            buf((2, NZ, R, SEQ)), buf((2, NZ, R, SEQ)), buf((2, NZ, R, SEQ), F32),
            buf((2, NZ, R, SEQ)), buf((2, NZ - 1, R, SEQ)), buf((2, R, SEQ), F32),
            buf((NA, 8, R, 128)), buf((NA, 2, 2, R, 128)), buf((NA, 2, 2, R, 128)),
            buf((NA, 2, 2, R, 128)), buf((NB, 2, 2, 80, 128)), buf((NB, 2, 2, 80, 128)),
            buf((8, 128), F32), buf((2, 8, 128), F32), buf((2, 8, 128), F32),
            buf((NA, XR, 128), F32), buf((NA, NY - 1, 32, 128)), buf((NA, NY - 1, 32, 128)),
            buf((NA, 192, 128)), buf((NA, 192, 128)), buf((NA, 192, 128), F32),
            buf((NB, NY, 160, 128)), buf((NB, 2, 3, 160, 128)), buf((NB, 160, 128), F32),
            buf((7, NB * 24, 128)), buf((7, NB * 24, 128)),
            buf((NX, 8, 128), F32), buf((NY, 8, 128), F32), buf((NH, 8, 128), F32),
            dma((6,)), dma((8,)), dma((6,)), dma((2,)), dma((16,)),
            dma((16,)), dma((16,)), dma((2,)), dma((2,)), dma((6,)), dma((6,)),
            dma((NA * 4,)), dma((NA * 4,)), dma((NB * 4,)), dma((NB * 4,)),
            dma((2,)), dma((2,)), dma((2,)), dma((2,)), dma((NA * 4,)), dma((NA * 4,)),
            dma((NA * 7,)), dma((NA * 7,)), dma((NA,)), dma((NA,)),
            dma((NB * 6,)), dma((NB * 6,)), dma((7,)), dma((7,)),
            dma((NX,)), dma((NX,)), dma((NY,)), dma((NY,)), dma((1,)), dma((NH,)),
        ],
        compiler_params=pltpu.CompilerParams(
            collective_id=0, has_side_effects=True, vmem_limit_bytes=60 * 2**20
        ),
        cost_estimate=pl.CostEstimate(
            flops=6 * 512 * D * F, bytes_accessed=3 * 2**20, transcendentals=2 * 512 * F
        ),
    )(layer_input.T, first_weight, hidden_grad, first_bias, other_squares)


def per_device(
    layer_input, first_weight, first_bias, hidden_grad, other_squares, weight_noise, bias_noise
):
    input_t, weight_sum, bias_sum = fused(
        layer_input, first_weight, hidden_grad, first_bias, other_squares
    )
    half = lax.axis_index("dp") % NH
    mine = lax.dynamic_slice_in_dim(weight_sum, half * 4, weight_noise.shape[0], 0)
    weight_grad = (mine + weight_noise) / EXAMPLES
    bias_grad = (bias_sum[: F // 128].reshape(F) + bias_noise) / EXAMPLES
    return (input_t.T, weight_grad, bias_grad)


def solution(mesh):
    placed = (P("dp", "mp"), P(None, "mp"), P("mp"), P("dp", "mp"), P("dp"), P("dp", "mp"), P("mp"))
    return jax.shard_map(
        per_device,
        mesh=mesh,
        in_specs=placed,
        out_specs=(P("dp", "mp"), P("dp", "mp"), P("mp")),
        check_vma=False,
    )
```
